32 devices in a mesh: ctx: 16 (over z, x, core), head: 2 (over y).
Axes of the slice: x: 2, y: 2, z: 4, core: 2. Of those that a mesh axis runs over, the one named last changes fastest.
Arguments:
- query: bfloat16 [3072, 1024], P('ctx', 'head'), may hold values from -16 to 16
- key: bfloat16 [3072, 256], P('ctx', 'head'), may hold values from -4 to 4
- value: bfloat16 [3072, 256], P('ctx', 'head'), may hold values from -6 to 6
- tangent_query: bfloat16 [3072, 1024], P('ctx', 'head'), may hold values from -6 to 6
- tangent_key: bfloat16 [3072, 256], P('ctx', 'head'), may hold values from -6 to 6
- tangent_value: bfloat16 [3072, 256], P('ctx', 'head'), may hold values from -6 to 6
- out_weight: bfloat16 [1024, 4096], P('head'), may hold values from -1.5 to 1.5
- block_order: int32 [32], replicated, may hold values from 0 to 31, as said below
Outputs:
- output: bfloat16 [3072, 4096], P(('ctx', 'head'))
- tangent_output: bfloat16 [3072, 4096], P(('ctx', 'head'))
The draws below stay inside these ranges and needn't reach their ends.
Inputs may be any that keep to these rules, and one draw needn't show every extreme that they name: block_order is a permutation in mirrored pairs: entries 2c and 2c + 1 sum to 2 * 16 - 1, so every stored pair of runs holds one early and one late run.
All inputs are finite; a program needn't handle non-finite values.
Results may differ from the reference program's by a relative error of at most 0.014.
Values may be sent and summed in bfloat16 or wider, within the bound.
No kernel may reach another device: no remote copies, remote signals or barrier semaphores. Data moves between devices by JAX's collectives and lax.ppermute only.
A program may use at most 64 MiB of HBM per device.

```python
import jax
import jax.numpy as jnp
from jax import lax

D = 4096
HD = 128
GROUP = 4
TOK_DEV = 192
KV = 2
HQ = 8
TOKENS = 3072
RUN = 96
N_CTX = 16


def paired_fields(key):
    keys = jax.random.truncated_normal(jax.random.fold_in(key, 11), -4.0, 4.0, (TOKENS, KV * HD), jnp.float32)
    queries = 1.5 * jax.random.truncated_normal(jax.random.fold_in(key, 14), -4.0, 4.0, (TOKENS, GROUP * KV * HD), jnp.float32)
    return (keys, queries)


def draw_key(key, part):
    return paired_fields(key)[0].astype(jnp.bfloat16)


def draw_query(key, part):
    return paired_fields(key)[1].astype(jnp.bfloat16)


def draw_block_order(key, part):
    early = jax.random.permutation(jax.random.fold_in(key, 21), N_CTX).astype(jnp.int32)
    late = (2 * N_CTX - 1 - early).astype(jnp.int32)
    return jnp.stack([early, late], axis=1).reshape(2 * N_CTX).astype(jnp.int32)


def shard_levels(key, dims, cuts, least, largest):
    def one(dim, parts):
        heights = jax.random.uniform(jax.random.fold_in(jax.random.fold_in(key, 6), dim), (parts,), jnp.float32, least / len(cuts), largest / len(cuts))
        return jnp.repeat(jnp.exp(heights), dims[dim] // parts).reshape((-1,) + (1,) * (len(dims) - dim - 1))

    loudness = one(*cuts[0])
    for cut in cuts[1:]:
        loudness = loudness * one(*cut)
    return loudness


def bell_draw(key, extent, scale, bound, shards=(), held_as=jnp.bfloat16):
    loudness = shard_levels(key, extent, shards, -0.22, 0.18) if shards else 1.0
    array = jax.random.normal(key, extent, jnp.float32) * scale * loudness
    return jnp.minimum(jnp.maximum(array, -bound), bound).astype(held_as)


def setup_inputs(seed: int = 0) -> dict:
    key_list = jax.random.split(jax.random.key(seed), 9)
    query = draw_query(jax.random.fold_in(key_list[8], 71), 0)
    key = draw_key(jax.random.fold_in(key_list[8], 71), 0)
    value = bell_draw(key_list[2], (TOKENS, KV * HD), 1.0, 6.0, ((0, 16), (1, 2)))
    tangent_query = bell_draw(key_list[3], (TOKENS, HQ * HD), 1.0, 6.0, ((0, 16), (1, 2)))
    tangent_key = bell_draw(key_list[4], (TOKENS, KV * HD), 1.0, 6.0, ((0, 16), (1, 2)))
    tangent_value = bell_draw(key_list[5], (TOKENS, KV * HD), 1.0, 6.0, ((0, 16), (1, 2)))
    out_weight = bell_draw(key_list[6], (HQ * HD, D), (HQ * HD // 64) ** -0.5, 1.5, ((0, 2),))
    block_order = draw_block_order(jax.random.fold_in(key_list[8], 71), 0)
    return dict(query=query, key=key, value=value, tangent_query=tangent_query, tangent_key=tangent_key, tangent_value=tangent_value, out_weight=out_weight, block_order=block_order)


def reference(query, key, value, tangent_query, tangent_key, tangent_value, out_weight, block_order):
    heads = GROUP * KV
    rows = jnp.arange(TOKENS, dtype=jnp.int32)
    place = block_order[rows // RUN].astype(jnp.int32) * RUN + rows % RUN
    scale = HD ** -0.5

    def spread(field):
        return jnp.repeat(field.reshape(TOKENS, KV, HD).astype(jnp.float32), GROUP, axis=1)

    keys = spread(key)
    values = spread(value)
    tangent_keys = spread(tangent_key)
    tangent_values = spread(tangent_value)

    def one_block(index):
        start = (index * TOK_DEV).astype(jnp.int32)
        queries = lax.dynamic_slice_in_dim(query, start, TOK_DEV, 0).reshape(TOK_DEV, heads, HD).astype(jnp.float32)
        tangent_queries = lax.dynamic_slice_in_dim(tangent_query, start, TOK_DEV, 0).reshape(TOK_DEV, heads, HD).astype(jnp.float32)
        query_place = lax.dynamic_slice_in_dim(place, start, TOK_DEV, 0)
        visible = place[None, None, :] <= query_place[None, :, None]
        scores = jnp.einsum("qhd,khd->hqk", queries, keys) * scale
        peak = jnp.max(jnp.where(visible, scores, -1e30), axis=-1, keepdims=True)
        weights = jnp.where(visible, jnp.exp(scores - peak), 0.0)
        total = jnp.sum(weights, axis=-1)
        weights_b = lax.optimization_barrier(weights.astype(jnp.bfloat16)).astype(jnp.float32)
        slopes = (jnp.einsum("qhd,khd->hqk", tangent_queries, keys) + jnp.einsum("qhd,khd->hqk", queries, tangent_keys)) * scale
        product = weights * slopes
        shift = jnp.sum(product, axis=-1)
        product_b = lax.optimization_barrier(product.astype(jnp.bfloat16)).astype(jnp.float32)
        context = jnp.einsum("hqk,khd->hqd", weights_b, values) / total[..., None]
        mixed = jnp.einsum("hqk,khd->hqd", product_b, values) + jnp.einsum("hqk,khd->hqd", weights_b, tangent_values)
        tangent_context = mixed / total[..., None] - (shift / total)[..., None] * context
        attn_rows = context.astype(jnp.bfloat16).transpose(1, 0, 2).reshape(TOK_DEV, heads * HD)
        tangent_rows = tangent_context.astype(jnp.bfloat16).transpose(1, 0, 2).reshape(TOK_DEV, heads * HD)
        return attn_rows, tangent_rows

    attn, tangent_attn = lax.map(one_block, jnp.arange(TOKENS // TOK_DEV, dtype=jnp.int32))
    attn = attn.reshape(TOKENS, heads * HD)
    tangent_attn = tangent_attn.reshape(TOKENS, heads * HD)
    width = GROUP * HD

    def projected(left):
        summed = jnp.zeros((TOKENS, D), jnp.float32)
        for group_index in range(KV):
            cols = left[:, group_index * width:(group_index + 1) * width]
            weight_rows = out_weight[group_index * width:(group_index + 1) * width]
            partial_sum = jnp.dot(cols, weight_rows, preferred_element_type=jnp.float32)
            partial_sum = lax.optimization_barrier(partial_sum.astype(jnp.bfloat16)).astype(jnp.float32)
            summed = summed + partial_sum
        return summed.astype(jnp.bfloat16)

    return projected(attn), projected(tangent_attn)
```

```python
import functools

import jax
import jax.numpy as jnp
from jax import lax
from jax.experimental import pallas as pl
from jax.experimental.pallas import tpu as pltpu
from jax.sharding import PartitionSpec as P

HD = 128
LOG2E = 1.4426950408889634
LOWEST = -1e30
VMEM = pl.BlockSpec(memory_space=pltpu.VMEM)
SMEM = pl.BlockSpec(memory_space=pltpu.SMEM)


def lanes(column, width):
    return jnp.broadcast_to(column, (column.shape[0], width))


def attend_kernel(
    sizes, meta, order, query, tangent_query, *refs
):
    packs, run, group, chunk = sizes
    pack_refs = refs[:packs]
    first_ref, second_ref = refs[packs : packs + 2]
    line, top, total, shift, both, mixed = refs[packs + 2 :]
    scale = HD ** (-0.5)

    at = 2
    for ref in pack_refs:
        for block in range(ref.shape[0] // (2 * run)):
            source = meta[at]
            at += 1
            for half in range(2):
                place = order[2 * source + half]
                rows = pl.ds(pl.multiple_of(place * run, run), run)
                begin = (2 * block + half) * run
                line[rows, :] = ref[begin : begin + run, :]

    me = meta[0]
    for step, out in enumerate((first_ref, second_ref)):
        half = meta[1] if step == 0 else 1 - meta[1]
        place = order[2 * me + half]
        rows = pl.ds(pl.multiple_of(half * run, run), run)
        q = [query[rows, h * HD : (h + 1) * HD] for h in range(group)]
        tq = [tangent_query[rows, h * HD : (h + 1) * HD] for h in range(group)]
        q = jnp.concatenate(q, axis=0)
        tq_q = jnp.concatenate([jnp.concatenate(tq, axis=0), q], axis=1)
        height = group * run
        top[...] = jnp.full(top.shape, LOWEST, jnp.float32)
        total[...] = jnp.zeros(total.shape, jnp.float32)
        shift[...] = jnp.zeros(shift.shape, jnp.float32)
        both[...] = jnp.zeros(both.shape, jnp.float32)
        mixed[...] = jnp.zeros(mixed.shape, jnp.float32)

        def visit(index, masked):
            cols = pl.ds(pl.multiple_of(index * chunk, chunk), chunk)
            keys = line[cols, 0:HD]
            keys_both = line[cols, 0 : 2 * HD]
            values = line[cols, 2 * HD : 3 * HD]
            values_both = line[cols, 2 * HD : 4 * HD]
            nt = (((1,), (1,)), ((), ()))
            scores = lax.dot_general(q, keys, nt, preferred_element_type=jnp.float32)
            scores = scores * (scale * LOG2E)
            if masked:
                col = index * chunk + lax.broadcasted_iota(jnp.int32, (height, chunk), 1)
                row = lax.rem(lax.broadcasted_iota(jnp.int32, (height, chunk), 0), run)
                scores = jnp.where(col <= place * run + row, scores, LOWEST)
            old = top[...]
            new = jnp.maximum(old, lanes(jnp.max(scores, axis=1, keepdims=True), HD))
            factor = jnp.exp2(old - new)
            top[...] = new
            weights = jnp.exp2(scores - jnp.tile(new, (1, chunk // HD)))
            slopes = lax.dot_general(tq_q, keys_both, nt, preferred_element_type=jnp.float32)
            product = weights * slopes
            weights_b = weights.astype(jnp.bfloat16)
            product_b = product.astype(jnp.bfloat16)
            part = weights[:, 0:HD]
            part_shift = product[:, 0:HD]
            for k in range(1, chunk // HD):
                part = part + weights[:, k * HD : (k + 1) * HD]
                part_shift = part_shift + product[:, k * HD : (k + 1) * HD]
            total[...] = total[...] * factor + part
            shift[...] = shift[...] * factor + part_shift
            both[...] = both[...] * jnp.tile(factor, (1, 2)) + jnp.dot(
                weights_b, values_both, preferred_element_type=jnp.float32
            )
            mixed[...] = mixed[...] * factor + jnp.dot(
                product_b, values, preferred_element_type=jnp.float32
            )

        whole = place * run // chunk

        @pl.loop(0, whole)
        def _(index):
            visit(index, False)

        visit(whole, True)
        inverse = lanes(1.0 / jnp.sum(total[...], axis=1, keepdims=True), HD)
        shifted = lanes(jnp.sum(shift[...], axis=1, keepdims=True), HD) * (scale * inverse)
        context = both[:, 0:HD] * inverse
        tangent = (mixed[...] * scale + both[:, HD : 2 * HD]) * inverse - shifted * context
        for h in range(group):
            out[0:run, h * HD : (h + 1) * HD] = context[h * run : (h + 1) * run].astype(out.dtype)
            out[run : 2 * run, h * HD : (h + 1) * HD] = tangent[h * run : (h + 1) * run].astype(
                out.dtype
            )


def attend(meta, order, query, tangent_query, packs):
    rows, width = query.shape
    run, group = rows // 2, width // HD
    count = sum(pack.shape[0] for pack in packs)
    chunk = 4 * run
    height = group * run
    out = jax.ShapeDtypeStruct((rows, width), jnp.bfloat16)
    sizes = (len(packs), run, group, chunk)
    flops = 2 * height * count * HD * 6
    return pl.pallas_call(
        functools.partial(attend_kernel, sizes),
        out_shape=(out, out),
        in_specs=[SMEM, SMEM] + [VMEM] * (2 + len(packs)),
        out_specs=(VMEM, VMEM),
        scratch_shapes=[
            pltpu.VMEM((count, 4 * HD), jnp.bfloat16),
            pltpu.VMEM((height, HD), jnp.float32),
            pltpu.VMEM((height, HD), jnp.float32),
            pltpu.VMEM((height, HD), jnp.float32),
            pltpu.VMEM((height, 2 * HD), jnp.float32),
            pltpu.VMEM((height, HD), jnp.float32),
        ],
        compiler_params=pltpu.CompilerParams(vmem_limit_bytes=40 * 2**20),
        cost_estimate=pl.CostEstimate(
            flops=flops, bytes_accessed=count * 8 * HD, transcendentals=height * count
        ),
        name="attend",
    )(meta, order, query, tangent_query, *packs)


def project_own_kernel(left, weight, out):
    out[...] = jnp.dot(left[...], weight[...], preferred_element_type=jnp.float32).astype(out.dtype)


def project_own(left, weight, tile=512):
    rows, depth = left.shape
    width = weight.shape[1]
    return pl.pallas_call(
        project_own_kernel,
        out_shape=jax.ShapeDtypeStruct((rows, width), jnp.bfloat16),
        grid=(width // tile,),
        in_specs=[
            pl.BlockSpec((rows, depth), lambda k: (0, 0)),
            pl.BlockSpec((depth, tile), lambda k: (0, k)),
        ],
        out_specs=pl.BlockSpec((rows, tile), lambda k: (0, k)),
        compiler_params=pltpu.CompilerParams(vmem_limit_bytes=20 * 2**20),
        cost_estimate=pl.CostEstimate(
            flops=2 * rows * depth * width, bytes_accessed=2 * depth * width, transcendentals=0
        ),
        name="project_own",
    )(left, weight)


def project_other_kernel(starts, left, partial, *refs):
    pieces, (out, tangent_out) = refs[:-2], refs[-2:]
    run = left.shape[0] // 2
    left = left[...]
    for n, piece in enumerate(pieces):
        width = piece.shape[1]
        cols = pl.ds(pl.multiple_of(starts[n], HD), width)
        other = jnp.dot(left, piece[...], preferred_element_type=jnp.float32)
        other = other.astype(jnp.bfloat16).astype(jnp.float32)
        sums = (partial[:, cols].astype(jnp.float32) + other).astype(out.dtype)
        out[:, cols] = sums[0:run]
        tangent_out[:, cols] = sums[run : 2 * run]


def project_other(starts, left, partial, pieces):
    rows = left.shape[0]
    width = partial.shape[1]
    out = jax.ShapeDtypeStruct((rows // 2, width), jnp.bfloat16)
    return pl.pallas_call(
        project_other_kernel,
        out_shape=(out, out),
        in_specs=[SMEM] + [VMEM] * (2 + len(pieces)),
        out_specs=(VMEM, VMEM),
        compiler_params=pltpu.CompilerParams(vmem_limit_bytes=40 * 2**20),
        cost_estimate=pl.CostEstimate(
            flops=2 * rows * left.shape[1] * width,
            bytes_accessed=2 * left.shape[1] * width,
            transcendentals=0,
        ),
        name="project_other",
    )(starts, left, partial, *pieces)


def whole_program(
    query, key, value, tangent_query, tangent_key, tangent_value, out_weight, block_order, axes
):
    run = query.shape[0] // 2
    pack = jnp.concatenate([key, tangent_key, value, tangent_value], axis=1)
    gathered = lax.all_gather(pack, "ctx", axis=0, tiled=True)
    me = lax.axis_index("ctx").astype(jnp.int32)
    meta = jnp.concatenate(
        [jnp.stack([me, jnp.int32(0)]), jnp.arange(axes["ctx"], dtype=jnp.int32)]
    )
    first, second = attend(meta, block_order, query, tangent_query, [gathered])
    left = jnp.concatenate([first[:run], second[:run], first[run:], second[run:]], axis=0)
    partial = project_own(left, out_weight)
    both = jnp.concatenate([partial[: 2 * run], partial[2 * run :]], axis=1)
    summed = lax.psum_scatter(both, "head", scatter_dimension=0, tiled=True)
    width = out_weight.shape[1]
    return summed[:, :width], summed[:, width:]


def paired_program(
    query, key, value, tangent_query, tangent_key, tangent_value, out_weight, block_order, axes
):
    count = axes["ctx"]
    width = out_weight.shape[1]
    me = lax.axis_index("ctx").astype(jnp.int32)
    side = lax.axis_index("head").astype(jnp.int32)

    def swap(array, bits):
        return lax.ppermute(array, "ctx", [(i, i ^ bits) for i in range(count)])

    def cross(array):
        return lax.ppermute(array, "head", [(0, 1), (1, 0)])

    core, level = me & 1, (me >> 2) & 1
    quarter, eighth = width // 4, width // 8
    direct_start = core * quarter
    shared_start = width // 2 + (2 * level + core) * eighth
    shared = cross(lax.dynamic_slice_in_dim(out_weight, shared_start, eighth, 1))
    direct = cross(lax.dynamic_slice_in_dim(out_weight, direct_start, quarter, 1))

    pack = jnp.concatenate([key, tangent_key, value, tangent_value], axis=1)
    bits, packs = [0], [pack]
    for step in (4, 8, 12):
        bits.append(step)
        packs.append(swap(pack, step))
    for n in range(4):
        bits.append(bits[n] ^ 2)
        packs.append(swap(packs[n], 2))
    for n in range(8):
        bits.append(bits[n] ^ 1)
        packs.append(swap(packs[n], 1))
    meta = jnp.stack([me, 1 - side] + [me ^ b for b in bits])
    theirs, mine = attend(meta, block_order, query, tangent_query, packs)

    shared_z = swap(shared, 4)
    pieces = [direct, swap(direct, 1), shared, shared_z, swap(shared, 1), swap(shared_z, 1)]
    half = width // 2
    starts = jnp.stack(
        [
            direct_start,
            (1 - core) * quarter,
            half + (2 * level + core) * eighth,
            half + (2 * (1 - level) + core) * eighth,
            half + (2 * level + 1 - core) * eighth,
            half + (2 * (1 - level) + 1 - core) * eighth,
        ]
    )
    other = cross(theirs)
    partial = project_own(mine, out_weight)
    return project_other(starts, other, partial, pieces)


def solution(mesh):
    axes = dict(mesh.shape)
    program = paired_program if axes == {"ctx": 16, "head": 2} else whole_program
    in_specs = (
        P("ctx", "head"),
        P("ctx", "head"),
        P("ctx", "head"),
        P("ctx", "head"),
        P("ctx", "head"),
        P("ctx", "head"),
        P("head", None),
        P(),
    )
    out_specs = (P(("ctx", "head"), None), P(("ctx", "head"), None))
    return jax.shard_map(
        functools.partial(program, axes=axes),
        mesh=mesh,
        in_specs=in_specs,
        out_specs=out_specs,
        check_vma=False,
    )
```

```python
import functools

import jax
import jax.numpy as jnp
from jax import lax
from jax.experimental import pallas as pl
from jax.experimental.pallas import tpu as pltpu
from jax.sharding import PartitionSpec as P

HD = 128
LOG2E = 1.4426950408889634
LOWEST = -1e30
VMEM = pl.BlockSpec(memory_space=pltpu.VMEM)
SMEM = pl.BlockSpec(memory_space=pltpu.SMEM)
ANY = pl.BlockSpec(memory_space=pl.ANY)
HBM = pl.BlockSpec(memory_space=pltpu.HBM)


def in_hbm(arrays):
    return [pltpu.with_memory_space_constraint(array, pltpu.HBM) for array in arrays]


def lanes(column, width):
    return jnp.broadcast_to(column, (column.shape[0], width))


SMALL = pl.CostEstimate(flops=1, bytes_accessed=1, transcendentals=0)
NT = (((1,), (1,)), ((), ()))


def attend_kernel(sizes, meta, query, tangent_query, *refs):
    packs, carried, last, held, run, group, chunk = sizes
    height = group * run
    pack_refs, refs = refs[:packs], refs[packs:]
    before, refs = refs[: 5 * carried], refs[5 * carried :]
    outs, refs = (refs[:2], refs[2:]) if last else (refs[:5], refs[5:])
    line, top, total, shift, both, mixed, sems = refs
    state = (top, total, shift, both, mixed)
    scale = HD ** (-0.5)

    copies = []
    blocks = [(ref, begin) for ref in pack_refs for begin in range(0, ref.shape[0], run)]
    for n, (ref, begin) in enumerate(blocks):
        rows = pl.ds(pl.multiple_of(meta[4 + n] * run, run), run)
        block = ref.at[begin : begin + run, :]
        if held:
            line[rows, :] = block[...]
        else:
            copies.append(pltpu.make_async_copy(block, line.at[rows, :], sems.at[n]))
            copies[-1].start()
    for copy in copies:
        copy.wait()

    own = meta[1]
    for step in range(2):
        half = meta[0] if step == 0 else 1 - meta[0]
        ahead = meta[2 + half]
        mine = slice(step * height, (step + 1) * height)
        rows = pl.ds(pl.multiple_of(half * run, run), run)
        q = [query[rows, h * HD : (h + 1) * HD] for h in range(group)]
        tq = [tangent_query[rows, h * HD : (h + 1) * HD] for h in range(group)]
        q = jnp.concatenate(q, axis=0)
        tq_q = jnp.concatenate([jnp.concatenate(tq, axis=0), q], axis=1)
        if carried:
            for now, then in zip(state, before):
                now[...] = then[mine, :]
        else:
            top[...] = jnp.full(top.shape, LOWEST, jnp.float32)
            for now in state[1:]:
                now[...] = jnp.zeros(now.shape, jnp.float32)

        def visit(index, masked):
            cols = pl.ds(pl.multiple_of(index * chunk, chunk), chunk)
            keys = line[cols, 0:HD]
            keys_both = line[cols, 0 : 2 * HD]
            values = line[cols, 2 * HD : 3 * HD]
            values_both = line[cols, 2 * HD : 4 * HD]
            scores = lax.dot_general(q, keys, NT, preferred_element_type=jnp.float32)
            scores = scores * (scale * LOG2E)
            if masked:
                col = index * chunk + lax.broadcasted_iota(jnp.int32, (height, chunk), 1)
                row = lax.rem(lax.broadcasted_iota(jnp.int32, (height, chunk), 0), run)
                scores = jnp.where(col < ahead * run + (row + 1) * own, scores, LOWEST)
            old = top[...]
            new = jnp.maximum(old, lanes(jnp.max(scores, axis=1, keepdims=True), HD))
            factor = jnp.exp2(old - new)
            top[...] = new
            weights = jnp.exp2(scores - jnp.tile(new, (1, chunk // HD)))
            slopes = lax.dot_general(tq_q, keys_both, NT, preferred_element_type=jnp.float32)
            product = weights * slopes
            weights_b = weights.astype(jnp.bfloat16)
            product_b = product.astype(jnp.bfloat16)
            part = weights[:, 0:HD]
            part_shift = product[:, 0:HD]
            for k in range(1, chunk // HD):
                part = part + weights[:, k * HD : (k + 1) * HD]
                part_shift = part_shift + product[:, k * HD : (k + 1) * HD]
            total[...] = total[...] * factor + part
            shift[...] = shift[...] * factor + part_shift
            both[...] = both[...] * jnp.tile(factor, (1, 2)) + jnp.dot(
                weights_b, values_both, preferred_element_type=jnp.float32
            )
            mixed[...] = mixed[...] * factor + jnp.dot(
                product_b, values, preferred_element_type=jnp.float32
            )

        whole = ahead * run // chunk

        @pl.loop(0, whole)
        def _(index):
            visit(index, False)

        @pl.when((ahead + own) * run > whole * chunk)
        def _():
            visit(whole, True)

        if not last:
            for now, out in zip(state, outs):
                out[mine, :] = now[...]
            continue
        inverse = lanes(1.0 / jnp.sum(total[...], axis=1, keepdims=True), HD)
        shifted = lanes(jnp.sum(shift[...], axis=1, keepdims=True), HD) * (scale * inverse)
        context = both[:, 0:HD] * inverse
        tangent = (mixed[...] * scale + both[:, HD : 2 * HD]) * inverse - shifted * context
        out = outs[step]
        for h in range(group):
            cols = slice(h * HD, (h + 1) * HD)
            head = slice(h * run, (h + 1) * run)
            out[0:run, cols] = context[head].astype(out.dtype)
            out[run : 2 * run, cols] = tangent[head].astype(out.dtype)


def ranks(order, first, me, sources, own):
    place = order.reshape(-1, 2)[sources].reshape(-1)
    rank = jnp.sum(place[None, :] < place[:, None], axis=1, dtype=jnp.int32)
    ours = lax.dynamic_slice_in_dim(order, 2 * me, 2)
    ahead = jnp.sum(place[None, :] < ours[:, None], axis=1, dtype=jnp.int32)
    return jnp.concatenate([jnp.stack([first, jnp.int32(own)]), ahead, rank])


def attend(meta, query, tangent_query, packs, before=(), last=True, held=False):
    rows, width = query.shape
    run, group = rows // 2, width // HD
    count = sum(pack.shape[0] for pack in packs)
    height = group * run
    chunk = 4 * run
    widths = (HD, HD, HD, 2 * HD, HD)
    if last:
        outs = (jax.ShapeDtypeStruct((rows, width), jnp.bfloat16),) * 2
    else:
        outs = tuple(jax.ShapeDtypeStruct((2 * height, w), jnp.float32) for w in widths)
    sizes = (len(packs), len(before) // 5, last, held, run, group, chunk)
    return pl.pallas_call(
        functools.partial(attend_kernel, sizes),
        out_shape=outs,
        in_specs=[SMEM, VMEM, VMEM] + [VMEM if held else ANY] * len(packs) + [VMEM] * len(before),
        out_specs=(VMEM,) * len(outs),
        scratch_shapes=[pltpu.VMEM((count, 4 * HD), jnp.bfloat16)]
        + [pltpu.VMEM((height, w), jnp.float32) for w in widths]
        + [pltpu.SemaphoreType.DMA((count // run,))],
        compiler_params=pltpu.CompilerParams(vmem_limit_bytes=16 * 2**20),
        cost_estimate=SMALL,
        name="attend_last" if last else "attend_early",
    )(meta, query, tangent_query, *(packs if held else in_hbm(packs)), *before)


def project_own_kernel(tile, left, weight, out, held, sems):
    count = weight.shape[1] // tile
    copies = []
    for n in range(count):
        cols = slice(n * tile, (n + 1) * tile)
        copies.append(pltpu.make_async_copy(weight.at[:, cols], held.at[n], sems.at[n]))
        copies[-1].start()
    rows = left[...]
    for n in range(count):
        copies[n].wait()
        out[:, n * tile : (n + 1) * tile] = jnp.dot(
            rows, held[n], preferred_element_type=jnp.float32
        ).astype(out.dtype)


def project_own(left, weight, tile=512):
    rows, depth = left.shape
    width = weight.shape[1]
    return pl.pallas_call(
        functools.partial(project_own_kernel, tile),
        out_shape=jax.ShapeDtypeStruct((rows, width), jnp.bfloat16),
        in_specs=[VMEM, HBM],
        out_specs=VMEM,
        scratch_shapes=[
            pltpu.VMEM((width // tile, depth, tile), jnp.bfloat16),
            pltpu.SemaphoreType.DMA((width // tile,)),
        ],
        compiler_params=pltpu.CompilerParams(vmem_limit_bytes=8 * 2**20),
        cost_estimate=SMALL,
        name="project_own",
    )(left, *in_hbm([weight]))


def project_other_kernel(counts, early, ours, starts, left, partial, *refs):
    pieces, refs = refs[: len(counts)], refs[len(counts) + 2 * ours :]
    outs, held, sums, (sems, out_sems) = refs[:2], refs[2 : 2 + early], refs[2 + early : -2], refs[-2:]
    copies = []
    for n in range(early):
        copies.append(pltpu.make_async_copy(pieces[n], held[n], sems.at[n]))
        copies[-1].start()
    run = left.shape[0] // 2
    rows = left[...]
    stores = []
    for n in list(range(early, len(counts))) + list(range(early)):
        piece = pieces[n]
        if n < early:
            copies[n].wait()
            piece = held[n]
        other = jnp.dot(rows, piece[...], preferred_element_type=jnp.float32)
        other = other.astype(jnp.bfloat16).astype(jnp.float32)
        width = piece.shape[1] // counts[n]
        for m in range(counts[n]):
            cols = pl.ds(pl.multiple_of(starts[sum(counts[:n]) + m], HD), width)
            here = slice(m * width, (m + 1) * width)
            sums[n][:, here] = (partial[:, cols].astype(jnp.float32) + other[:, here]).astype(
                jnp.bfloat16
            )
            for k in range(2):
                stores.append(
                    pltpu.make_async_copy(
                        sums[n].at[k * run : (k + 1) * run, here],
                        outs[k].at[:, cols],
                        out_sems.at[sum(counts[:n]) + m, k],
                    )
                )
                stores[-1].start()
    for store in stores:
        store.wait()


def project_other(starts, left, partial, early, late, outs=()):
    rows = left.shape[0]
    width = partial.shape[1]
    out = jax.ShapeDtypeStruct((rows // 2, width), jnp.bfloat16)
    pieces = early + late
    counts = tuple(len(some) for some in starts)
    starts = jnp.stack([start for some in starts for start in some])
    return pl.pallas_call(
        functools.partial(project_other_kernel, counts, len(early), int(bool(outs))),
        out_shape=(out, out),
        in_specs=[SMEM, VMEM, VMEM] + [ANY] * len(early) + [VMEM] * len(late) + [HBM] * len(outs),
        out_specs=(HBM, HBM),
        input_output_aliases={3 + len(pieces) + n: n for n in range(len(outs))},
        scratch_shapes=[pltpu.VMEM(piece.shape, piece.dtype) for piece in early]
        + [pltpu.VMEM((rows, piece.shape[1]), jnp.bfloat16) for piece in pieces]
        + [pltpu.SemaphoreType.DMA((max(len(early), 1),))]
        + [pltpu.SemaphoreType.DMA((sum(counts), 2))],
        compiler_params=pltpu.CompilerParams(vmem_limit_bytes=16 * 2**20),
        cost_estimate=SMALL,
        name="project_other",
    )(starts, left, partial, *in_hbm(early), *late, *outs)


def whole_program(
    query, key, value, tangent_query, tangent_key, tangent_value, out_weight, block_order, axes
):
    run = query.shape[0] // 2
    pack = jnp.concatenate([key, tangent_key, value, tangent_value], axis=1)
    gathered = lax.all_gather(pack, "ctx", axis=0, tiled=True)
    me = lax.axis_index("ctx").astype(jnp.int32)
    meta = ranks(block_order, jnp.int32(0), me, jnp.arange(axes["ctx"], dtype=jnp.int32), 1)
    first, second = attend(meta, query, tangent_query, [gathered])
    left = jnp.concatenate([first[:run], second[:run], first[run:], second[run:]], axis=0)
    partial = project_own(left, out_weight)
    both = jnp.concatenate([partial[: 2 * run], partial[2 * run :]], axis=1)
    summed = lax.psum_scatter(both, "head", scatter_dimension=0, tiled=True)
    width = out_weight.shape[1]
    return summed[:, :width], summed[:, width:]


def stage_kernel(widths, starts, key, tangent_key, value, tangent_value, weight, pack, *refs):
    parts, sems = refs[:-1], refs[-1]
    moves = []
    for part, some in zip(parts, widths):
        at = 0
        for width in some:
            source = weight.at[:, pl.ds(pl.multiple_of(starts[len(moves)], HD), width)]
            moves.append((source, part.at[:, at : at + width]))
            at += width
    for n, field in enumerate((key, tangent_key, value, tangent_value)):
        moves.append((field, pack.at[:, n * HD : (n + 1) * HD]))
    copies = [pltpu.make_async_copy(*move, sems.at[n]) for n, move in enumerate(moves)]
    for copy in copies:
        copy.start()
    for copy in copies:
        copy.wait()


def stage(starts, fields, weight, widths):
    rows, depth = fields[0].shape[0], weight.shape[0]
    return pl.pallas_call(
        functools.partial(stage_kernel, widths),
        out_shape=[jax.ShapeDtypeStruct((rows, 4 * HD), jnp.bfloat16)]
        + [jax.ShapeDtypeStruct((depth, sum(some)), jnp.bfloat16) for some in widths],
        in_specs=[SMEM] + [HBM] * 5,
        out_specs=[VMEM] * (1 + len(widths)),
        scratch_shapes=[pltpu.SemaphoreType.DMA((4 + sum(len(some) for some in widths),))],
        compiler_params=pltpu.CompilerParams(vmem_limit_bytes=4 * 2**20),
        name="stage",
    )(starts, *in_hbm((*fields, weight)))


def paired_program(
    query, key, value, tangent_query, tangent_key, tangent_value, out_weight, block_order, axes
):
    count = axes["ctx"]
    width = out_weight.shape[1]
    me = lax.axis_index("ctx").astype(jnp.int32)
    side = lax.axis_index("head").astype(jnp.int32)

    def swap(array, bits, *after):
        if after:
            array = lax.optimization_barrier((array,) + after)[0]
        return lax.ppermute(array, "ctx", [(i, i ^ bits) for i in range(count)])

    def cross(array):
        return lax.ppermute(array, "head", [(0, 1), (1, 0)])

    core, column, level = me & 1, (me >> 1) & 1, (me >> 2) & 1
    part = width // 16

    def by_level(level, core):
        return (2 * level + core) * part

    def by_column(column, core):
        return (4 + 2 * column + core) * part

    def by_core(core):
        return (8 + 4 * core) * part

    pack, shared, direct = stage(
        jnp.stack([by_level(level, core), by_column(column, core), by_core(core)]),
        (key, tangent_key, value, tangent_value),
        out_weight,
        ((part, part), (4 * part,)),
    )
    tie = lax.optimization_barrier
    bits = ([0, 1, 2, 4, 8, 3, 5, 9], [6, 12, 10, 7, 13, 11], [14, 15])
    metas = [
        ranks(block_order, 1 - side, me, me ^ jnp.array(some, jnp.int32), int(0 in some))
        for some in bits
    ]

    shared = cross(shared)
    c0, x0, z1, z2 = swap(pack, 1), swap(pack, 2), swap(pack, 4), swap(pack, 8)
    metas, pack, c0, x0, z1, z2, direct = tie((metas, pack, c0, x0, z1, z2, direct))
    direct = cross(direct)
    cx0, cz1, cz2 = swap(x0, 1), swap(z1, 1), swap(z2, 1)
    x1, z3, x2 = swap(z1, 2), swap(z2, 4), swap(z2, 2)
    packs = [pack, c0, x0, z1, z2, cx0, cz1, cz2]
    state = attend(metas[0], query, tangent_query, packs, last=False)
    level_part, column_part = shared[:, :part], shared[:, part:]
    x1, x2, z3, shared, level_part, column_part, state = tie(
        (x1, x2, z3, shared, level_part, column_part, state)
    )
    x3 = swap(z3, 2)
    cx1, cz3, cx2 = swap(x1, 1), swap(z3, 1), swap(x2, 1)
    packs = [x1, z3, x2, cx1, cz3, cx2]
    state = attend(metas[1], query, tangent_query, packs, state, last=False, held=True)
    x3, shared, level_part, column_part, state = tie((x3, shared, level_part, column_part, state))
    level_part, column_part = swap(level_part, 4), swap(column_part, 2)
    cx3, shared_core = tie((swap(x3, 1), swap(shared, 1)))
    theirs, mine = attend(metas[2], query, tangent_query, [x3, cx3], state, held=True)

    other, partial, level_part, column_part, direct = tie(
        (cross(theirs), project_own(mine, out_weight), level_part, column_part, direct)
    )
    far = [swap(p, 1) for p in (direct, level_part, column_part)]
    outs = project_other(
        [
            [by_level(level, core), by_column(column, core)],
            [by_level(1 - level, core)],
            [by_column(1 - column, core)],
            [by_core(core)],
            [by_level(level, 1 - core), by_column(column, 1 - core)],
        ],
        other,
        partial,
        [shared, level_part, column_part, direct],
        [shared_core],
    )
    return project_other(
        [[by_core(1 - core)], [by_level(1 - level, 1 - core)], [by_column(1 - column, 1 - core)]],
        other,
        partial,
        [],
        far,
        outs,
    )


def solution(mesh):
    axes = dict(mesh.shape)
    program = paired_program if axes == {"ctx": 16, "head": 2} else whole_program
    in_specs = (
        P("ctx", "head"),
        P("ctx", "head"),
        P("ctx", "head"),
        P("ctx", "head"),
        P("ctx", "head"),
        P("ctx", "head"),
        P("head", None),
        P(),
    )
    out_specs = (P(("ctx", "head"), None), P(("ctx", "head"), None))
    return jax.shard_map(
        functools.partial(program, axes=axes),
        mesh=mesh,
        in_specs=in_specs,
        out_specs=out_specs,
        check_vma=False,
    )
```

```python
import functools

import jax
import jax.numpy as jnp
from jax import lax
from jax.experimental import pallas as pl
from jax.experimental.pallas import tpu as pltpu
from jax.sharding import PartitionSpec as P

HD = 128
LOG2E = 1.4426950408889634
LOWEST = -1e30
VMEM = pl.BlockSpec(memory_space=pltpu.VMEM)
SMEM = pl.BlockSpec(memory_space=pltpu.SMEM)
ANY = pl.BlockSpec(memory_space=pl.ANY)
HBM = pl.BlockSpec(memory_space=pltpu.HBM)


def in_hbm(arrays):
    return [pltpu.with_memory_space_constraint(array, pltpu.HBM) for array in arrays]


def lanes(column, width):
    return jnp.broadcast_to(column, (column.shape[0], width))


SMALL = pl.CostEstimate(flops=1, bytes_accessed=1, transcendentals=0)
LARGE = pl.CostEstimate(flops=10**11, bytes_accessed=1, transcendentals=0)
NT = (((1,), (1,)), ((), ()))


def attend_kernel(sizes, meta, query, tangent_query, *refs):
    packs, carried, last, held, run, group, chunk = sizes
    height = group * run
    pack_refs, refs = refs[:packs], refs[packs:]
    before, refs = refs[: 5 * carried], refs[5 * carried :]
    outs, refs = (refs[:2], refs[2:]) if last else (refs[:5], refs[5:])
    line, top, total, shift, both, mixed, sems = refs
    state = (top, total, shift, both, mixed)
    scale = HD ** (-0.5)

    copies = []
    blocks = [(ref, begin) for ref in pack_refs for begin in range(0, ref.shape[0], run)]
    for n, (ref, begin) in enumerate(blocks):
        rows = pl.ds(pl.multiple_of(meta[4 + n] * run, run), run)
        block = ref.at[begin : begin + run, :]
        if held:
            line[rows, :] = block[...]
        else:
            copies.append(pltpu.make_async_copy(block, line.at[rows, :], sems.at[n]))
            copies[-1].start()
    for copy in copies:
        copy.wait()

    own = meta[1]
    for step in range(2):
        half = meta[0] if step == 0 else 1 - meta[0]
        ahead = meta[2 + half]
        mine = slice(step * height, (step + 1) * height)
        rows = pl.ds(pl.multiple_of(half * run, run), run)
        q = [query[rows, h * HD : (h + 1) * HD] for h in range(group)]
        tq = [tangent_query[rows, h * HD : (h + 1) * HD] for h in range(group)]
        q = jnp.concatenate(q, axis=0)
        tq_q = jnp.concatenate([jnp.concatenate(tq, axis=0), q], axis=1)
        if carried:
            for now, then in zip(state, before):
                now[...] = then[mine, :]
        else:
            top[...] = jnp.full(top.shape, LOWEST, jnp.float32)
            for now in state[1:]:
                now[...] = jnp.zeros(now.shape, jnp.float32)

        def visit(index, masked):
            cols = pl.ds(pl.multiple_of(index * chunk, chunk), chunk)
            keys = line[cols, 0:HD]
            keys_both = line[cols, 0 : 2 * HD]
            values = line[cols, 2 * HD : 3 * HD]
            values_both = line[cols, 2 * HD : 4 * HD]
            scores = lax.dot_general(q, keys, NT, preferred_element_type=jnp.float32)
            scores = scores * (scale * LOG2E)
            if masked:
                col = index * chunk + lax.broadcasted_iota(jnp.int32, (height, chunk), 1)
                row = lax.rem(lax.broadcasted_iota(jnp.int32, (height, chunk), 0), run)
                scores = jnp.where(col < ahead * run + (row + 1) * own, scores, LOWEST)
            old = top[...]
            new = jnp.maximum(old, lanes(jnp.max(scores, axis=1, keepdims=True), HD))
            factor = jnp.exp2(old - new)
            top[...] = new
            weights = jnp.exp2(scores - jnp.tile(new, (1, chunk // HD)))
            slopes = lax.dot_general(tq_q, keys_both, NT, preferred_element_type=jnp.float32)
            product = weights * slopes
            weights_b = weights.astype(jnp.bfloat16)
            product_b = product.astype(jnp.bfloat16)
            part = weights[:, 0:HD]
            part_shift = product[:, 0:HD]
            for k in range(1, chunk // HD):
                part = part + weights[:, k * HD : (k + 1) * HD]
                part_shift = part_shift + product[:, k * HD : (k + 1) * HD]
            total[...] = total[...] * factor + part
            shift[...] = shift[...] * factor + part_shift
            both[...] = both[...] * jnp.tile(factor, (1, 2)) + jnp.dot(
                weights_b, values_both, preferred_element_type=jnp.float32
            )
            mixed[...] = mixed[...] * factor + jnp.dot(
                product_b, values, preferred_element_type=jnp.float32
            )

        whole = ahead * run // chunk

        @pl.loop(0, whole)
        def _(index):
            visit(index, False)

        @pl.when((ahead + own) * run > whole * chunk)
        def _():
            visit(whole, True)

        if not last:
            for now, out in zip(state, outs):
                out[mine, :] = now[...]
            continue
        inverse = lanes(1.0 / jnp.sum(total[...], axis=1, keepdims=True), HD)
        shifted = lanes(jnp.sum(shift[...], axis=1, keepdims=True), HD) * (scale * inverse)
        context = both[:, 0:HD] * inverse
        tangent = (mixed[...] * scale + both[:, HD : 2 * HD]) * inverse - shifted * context
        out = outs[step]
        for h in range(group):
            cols = slice(h * HD, (h + 1) * HD)
            head = slice(h * run, (h + 1) * run)
            out[0:run, cols] = context[head].astype(out.dtype)
            out[run : 2 * run, cols] = tangent[head].astype(out.dtype)


def ranks(order, first, me, sources, own):
    place = order.reshape(-1, 2)[sources].reshape(-1)
    rank = jnp.sum(place[None, :] < place[:, None], axis=1, dtype=jnp.int32)
    ours = lax.dynamic_slice_in_dim(order, 2 * me, 2)
    ahead = jnp.sum(place[None, :] < ours[:, None], axis=1, dtype=jnp.int32)
    return jnp.concatenate([jnp.stack([first, jnp.int32(own)]), ahead, rank])


def attend(meta, query, tangent_query, packs, before=(), last=True, held=False):
    rows, width = query.shape
    run, group = rows // 2, width // HD
    count = sum(pack.shape[0] for pack in packs)
    height = group * run
    chunk = 4 * run
    widths = (HD, HD, HD, 2 * HD, HD)
    if last:
        outs = (jax.ShapeDtypeStruct((rows, width), jnp.bfloat16),) * 2
    else:
        outs = tuple(jax.ShapeDtypeStruct((2 * height, w), jnp.float32) for w in widths)
    sizes = (len(packs), len(before) // 5, last, held, run, group, chunk)
    return pl.pallas_call(
        functools.partial(attend_kernel, sizes),
        out_shape=outs,
        in_specs=[SMEM, VMEM, VMEM] + [VMEM if held else ANY] * len(packs) + [VMEM] * len(before),
        out_specs=(VMEM,) * len(outs),
        scratch_shapes=[pltpu.VMEM((count, 4 * HD), jnp.bfloat16)]
        + [pltpu.VMEM((height, w), jnp.float32) for w in widths]
        + [pltpu.SemaphoreType.DMA((count // run,))],
        compiler_params=pltpu.CompilerParams(vmem_limit_bytes=16 * 2**20),
        cost_estimate=SMALL,
        name="attend_last" if last else "attend_early",
    )(meta, query, tangent_query, *(packs if held else in_hbm(packs)), *before)


def project_own_kernel(tile, left, weight, out, held, sems):
    count = weight.shape[1] // tile
    copies = []
    for n in range(count):
        cols = slice(n * tile, (n + 1) * tile)
        copies.append(pltpu.make_async_copy(weight.at[:, cols], held.at[n], sems.at[n]))
        copies[-1].start()
    rows = left[...]
    for n in range(count):
        copies[n].wait()
        out[:, n * tile : (n + 1) * tile] = jnp.dot(
            rows, held[n], preferred_element_type=jnp.float32
        ).astype(out.dtype)


def project_own(left, weight, tile=512):
    rows, depth = left.shape
    width = weight.shape[1]
    return pl.pallas_call(
        functools.partial(project_own_kernel, tile),
        out_shape=jax.ShapeDtypeStruct((rows, width), jnp.bfloat16),
        in_specs=[VMEM, HBM],
        out_specs=VMEM,
        scratch_shapes=[
            pltpu.VMEM((width // tile, depth, tile), jnp.bfloat16),
            pltpu.SemaphoreType.DMA((width // tile,)),
        ],
        compiler_params=pltpu.CompilerParams(vmem_limit_bytes=8 * 2**20),
        cost_estimate=SMALL,
        name="project_own",
    )(left, *in_hbm([weight]))


def columns_at(starts, counts, n, width):
    width = width // counts[n]
    at = sum(counts[:n])
    return [
        (
            slice(m * width, (m + 1) * width),
            pl.ds(pl.multiple_of(starts[at + m], HD), width),
        )
        for m in range(counts[n])
    ]


def project_other_kernel(counts, early, done, starts, left, partial, *refs):
    total = len(counts)
    pieces, refs = refs[:total], refs[total:]
    outs, refs = (refs[:2], refs[2:]) if done else ([], refs)
    sums, refs = list(pieces[:done]) + list(refs[: total - done]), refs[total - done :]
    held, (sems, out_sems) = refs[:early], refs[early:]
    run = left.shape[0] // 2
    rows = left[...]
    copies, stores = [], []
    for n in range(early):
        copies.append(pltpu.make_async_copy(pieces[done + n], held[n], sems.at[n]))
        copies[-1].start()

    def store(n):
        if not done:
            return
        for m, (here, cols) in enumerate(columns_at(starts, counts, n, sums[n].shape[1])):
            for k in range(2):
                stores.append(
                    pltpu.make_async_copy(
                        sums[n].at[k * run : (k + 1) * run, here],
                        outs[k].at[:, cols],
                        out_sems.at[sum(counts[:n]) + m, k],
                    )
                )
                stores[-1].start()

    for n in range(done):
        store(n)
    for n in list(range(done + early, total)) + list(range(done, done + early)):
        piece = pieces[n]
        if n < done + early:
            copies[n - done].wait()
            piece = held[n - done]
        other = jnp.dot(rows, piece[...], preferred_element_type=jnp.float32)
        other = other.astype(jnp.bfloat16).astype(jnp.float32)
        for here, cols in columns_at(starts, counts, n, piece.shape[1]):
            sums[n][:, here] = (partial[:, cols].astype(jnp.float32) + other[:, here]).astype(
                jnp.bfloat16
            )
        store(n)
    for copy in stores:
        copy.wait()


def project_other(places, left, partial, early, late, done=()):
    rows, width = left.shape[0], partial.shape[1]
    pieces = early + late
    counts = tuple(len(some) for some in places)
    starts = jnp.stack([start for some in places for start in some])
    sums = [jax.ShapeDtypeStruct((rows, piece.shape[1]), jnp.bfloat16) for piece in pieces]
    out = jax.ShapeDtypeStruct((rows // 2, width), jnp.bfloat16)
    scratch = [pltpu.VMEM(some.shape, some.dtype) for some in sums] if done else []
    scratch = scratch + [pltpu.VMEM(piece.shape, piece.dtype) for piece in early]
    return pl.pallas_call(
        functools.partial(project_other_kernel, counts, len(early), len(done)),
        out_shape=[out, out] if done else sums,
        in_specs=[SMEM, VMEM, VMEM] + [VMEM] * len(done) + [ANY] * len(early) + [VMEM] * len(late),
        out_specs=[HBM, HBM] if done else [VMEM] * len(sums),
        scratch_shapes=scratch
        + [pltpu.SemaphoreType.DMA((max(len(early), 1),))]
        + [pltpu.SemaphoreType.DMA((len(starts), 2))],
        compiler_params=pltpu.CompilerParams(vmem_limit_bytes=16 * 2**20),
        cost_estimate=SMALL if done else LARGE,
        name="project_last" if done else "project_other",
    )(starts, left, partial, *done, *in_hbm(early), *late)


def whole_program(
    query, key, value, tangent_query, tangent_key, tangent_value, out_weight, block_order, axes
):
    run = query.shape[0] // 2
    pack = jnp.concatenate([key, tangent_key, value, tangent_value], axis=1)
    gathered = lax.all_gather(pack, "ctx", axis=0, tiled=True)
    me = lax.axis_index("ctx").astype(jnp.int32)
    meta = ranks(block_order, jnp.int32(0), me, jnp.arange(axes["ctx"], dtype=jnp.int32), 1)
    first, second = attend(meta, query, tangent_query, [gathered])
    left = jnp.concatenate([first[:run], second[:run], first[run:], second[run:]], axis=0)
    partial = project_own(left, out_weight)
    both = jnp.concatenate([partial[: 2 * run], partial[2 * run :]], axis=1)
    summed = lax.psum_scatter(both, "head", scatter_dimension=0, tiled=True)
    width = out_weight.shape[1]
    return summed[:, :width], summed[:, width:]


def stage_kernel(widths, count, starts, weight, *refs):
    fields, outs, sems = refs[:count], refs[count:-1], refs[-1]
    moves = [(field, outs[0].at[:, n * HD : (n + 1) * HD]) for n, field in enumerate(fields)]
    parts = outs[1:] if fields else outs
    for part, some in zip(parts, widths):
        at = 0
        for width in some:
            cols = pl.ds(pl.multiple_of(starts[len(moves) - count], HD), width)
            moves.append((weight.at[:, cols], part.at[:, at : at + width]))
            at += width
    copies = [pltpu.make_async_copy(*move, sems.at[n]) for n, move in enumerate(moves)]
    for copy in copies:
        copy.start()
    for copy in copies:
        copy.wait()


def stage(starts, weight, widths, fields=()):
    shapes = [(weight.shape[0], sum(some)) for some in widths]
    if fields:
        shapes = [(fields[0].shape[0], HD * len(fields))] + shapes
    return pl.pallas_call(
        functools.partial(stage_kernel, widths, len(fields)),
        out_shape=[jax.ShapeDtypeStruct(shape, jnp.bfloat16) for shape in shapes],
        in_specs=[SMEM] + [HBM] * (1 + len(fields)),
        out_specs=[VMEM] * len(shapes),
        scratch_shapes=[pltpu.SemaphoreType.DMA((len(fields) + len(starts),))],
        compiler_params=pltpu.CompilerParams(vmem_limit_bytes=4 * 2**20),
        cost_estimate=SMALL,
        name="stage",
    )(jnp.stack(starts), *in_hbm((weight, *fields)))


def paired_program(
    query, key, value, tangent_query, tangent_key, tangent_value, out_weight, block_order, axes
):
    count = axes["ctx"]
    width = out_weight.shape[1]
    me = lax.axis_index("ctx").astype(jnp.int32)
    side = lax.axis_index("head").astype(jnp.int32)

    def swap(array, bits, *after):
        if after:
            array = lax.optimization_barrier((array,) + after)[0]
        return lax.ppermute(array, "ctx", [(i, i ^ bits) for i in range(count)])

    def cross(array):
        return lax.ppermute(array, "head", [(0, 1), (1, 0)])

    core, column, level = me & 1, (me >> 1) & 1, (me >> 2) & 1
    part = width // 16

    def by_level(level, core):
        return (2 * level + core) * part

    def by_column(column, core):
        return (4 + 2 * column + core) * part

    def by_core(core):
        return (8 + 4 * core) * part

    fields = (key, tangent_key, value, tangent_value)
    places = [by_level(level, core), by_column(column, core)]
    pack, shared = stage(places, out_weight, ((part, part),), fields)
    (direct,) = stage([by_core(core)], out_weight, ((4 * part,),))
    tie = lax.optimization_barrier
    bits = ([0, 1, 2, 4, 8, 3, 5, 9], [6, 12, 10, 7, 13, 11], [14, 15])
    metas = [
        ranks(block_order, 1 - side, me, me ^ jnp.array(some, jnp.int32), int(0 in some))
        for some in bits
    ]

    c0, x0, z1, z2 = swap(pack, 1), swap(pack, 2), swap(pack, 4), swap(pack, 8)
    shared = cross(shared)
    metas, pack, c0, x0, z1, z2, direct = tie((metas, pack, c0, x0, z1, z2, direct))
    direct = cross(direct)
    cx0, cz1, cz2 = swap(x0, 1), swap(z1, 1), swap(z2, 1)
    x1, z3, x2 = swap(z1, 2), swap(z2, 4), swap(z2, 2)
    packs = [pack, c0, x0, z1, z2, cx0, cz1, cz2]
    state = attend(metas[0], query, tangent_query, packs, last=False)
    level_part, column_part = shared[:, :part], shared[:, part:]
    x1, x2, z3, shared, level_part, column_part, state = tie(
        (x1, x2, z3, shared, level_part, column_part, state)
    )
    x3 = swap(z3, 2)
    cx1, cz3, cx2 = swap(x1, 1), swap(z3, 1), swap(x2, 1)
    packs = [x1, z3, x2, cx1, cz3, cx2]
    state = attend(metas[1], query, tangent_query, packs, state, last=False, held=True)
    x3, shared, level_part, column_part, state = tie((x3, shared, level_part, column_part, state))
    level_part, column_part = swap(level_part, 4), swap(column_part, 2)
    cx3, shared_core = tie((swap(x3, 1), swap(shared, 1)))
    theirs, mine = attend(metas[2], query, tangent_query, [x3, cx3], state, held=True)

    other = cross(theirs)
    partial, level_part, column_part, direct = tie(
        (project_own(mine, out_weight), level_part, column_part, direct)
    )
    far = [swap(p, 1) for p in (direct, level_part, column_part)]
    near = [
        [by_level(level, core), by_column(column, core)],
        [by_level(level, 1 - core), by_column(column, 1 - core)],
        [by_level(1 - level, core)],
        [by_column(1 - column, core)],
        [by_core(core)],
    ]
    sums = project_other(
        near, other, partial, [shared, shared_core], [level_part, column_part, direct]
    )
    rest = [[by_core(1 - core)], [by_level(1 - level, 1 - core)], [by_column(1 - column, 1 - core)]]
    return tuple(project_other(near + rest, other, partial, [], far, sums))


def solution(mesh):
    axes = dict(mesh.shape)
    program = paired_program if axes == {"ctx": 16, "head": 2} else whole_program
    in_specs = (
        P("ctx", "head"),
        P("ctx", "head"),
        P("ctx", "head"),
        P("ctx", "head"),
        P("ctx", "head"),
        P("ctx", "head"),
        P("head", None),
        P(),
    )
    out_specs = (P(("ctx", "head"), None), P(("ctx", "head"), None))
    return jax.shard_map(
        functools.partial(program, axes=axes),
        mesh=mesh,
        in_specs=in_specs,
        out_specs=out_specs,
        check_vma=False,
    )
```

```python
import functools

import jax
import jax.numpy as jnp
from jax import lax
from jax.experimental import pallas as pl
from jax.experimental.pallas import tpu as pltpu
from jax.sharding import PartitionSpec as P

HD = 128
LOG2E = 1.4426950408889634
LOWEST = -1e30
VMEM = pl.BlockSpec(memory_space=pltpu.VMEM)
SMEM = pl.BlockSpec(memory_space=pltpu.SMEM)
ANY = pl.BlockSpec(memory_space=pl.ANY)
HBM = pl.BlockSpec(memory_space=pltpu.HBM)


def in_hbm(arrays):
    return [pltpu.with_memory_space_constraint(array, pltpu.HBM) for array in arrays]


def lanes(column, width):
    return jnp.broadcast_to(column, (column.shape[0], width))


SMALL = pl.CostEstimate(flops=1, bytes_accessed=1, transcendentals=0)
LARGE = pl.CostEstimate(flops=10**11, bytes_accessed=1, transcendentals=0)
NT = (((1,), (1,)), ((), ()))


def attend_kernel(sizes, meta, query, tangent_query, *refs):
    packs, carried, last, held, cuts, run, group, chunk = sizes
    height = group * run
    pack_refs, refs = refs[:packs], refs[packs:]
    before, refs = refs[: 5 * carried], refs[5 * carried :]
    whole_ref, refs = (refs[0], refs[1:]) if cuts else (None, refs)
    outs, refs = (refs[:2], refs[2:]) if last else (refs[:5], refs[5:])
    cut_refs, (line, top, total, shift, both, mixed, sems) = refs[:cuts], refs[cuts:]
    state = (top, total, shift, both, mixed)
    scale = HD ** (-0.5)

    aside, at = [], 0
    for n, ref in enumerate(cut_refs):
        source = whole_ref.at[:, at : at + ref.shape[1]]
        aside.append(pltpu.make_async_copy(source, ref, sems.at[line.shape[0] // run + n]))
        aside[-1].start()
        at += ref.shape[1]
    copies = []
    blocks = [(ref, begin) for ref in pack_refs for begin in range(0, ref.shape[0], run)]
    for n, (ref, begin) in enumerate(blocks):
        rows = pl.ds(pl.multiple_of(meta[4 + n] * run, run), run)
        block = ref.at[begin : begin + run, :]
        if held:
            line[rows, :] = block[...]
        else:
            copies.append(pltpu.make_async_copy(block, line.at[rows, :], sems.at[n]))
            copies[-1].start()
    for copy in copies:
        copy.wait()

    own = meta[1]
    for step in range(2):
        half = meta[0] if step == 0 else 1 - meta[0]
        ahead = meta[2 + half]
        mine = slice(step * height, (step + 1) * height)
        rows = pl.ds(pl.multiple_of(half * run, run), run)
        q = [query[rows, h * HD : (h + 1) * HD] for h in range(group)]
        tq = [tangent_query[rows, h * HD : (h + 1) * HD] for h in range(group)]
        q = jnp.concatenate(q, axis=0)
        tq_q = jnp.concatenate([jnp.concatenate(tq, axis=0), q], axis=1)
        if carried:
            for now, then in zip(state, before):
                now[...] = then[mine, :]
        else:
            top[...] = jnp.full(top.shape, LOWEST, jnp.float32)
            for now in state[1:]:
                now[...] = jnp.zeros(now.shape, jnp.float32)

        def visit(index, masked):
            cols = pl.ds(pl.multiple_of(index * chunk, chunk), chunk)
            keys = line[cols, 0:HD]
            keys_both = line[cols, 0 : 2 * HD]
            values = line[cols, 2 * HD : 3 * HD]
            values_both = line[cols, 2 * HD : 4 * HD]
            scores = lax.dot_general(q, keys, NT, preferred_element_type=jnp.float32)
            scores = scores * (scale * LOG2E)
            if masked:
                col = index * chunk + lax.broadcasted_iota(jnp.int32, (height, chunk), 1)
                row = lax.rem(lax.broadcasted_iota(jnp.int32, (height, chunk), 0), run)
                scores = jnp.where(col < ahead * run + (row + 1) * own, scores, LOWEST)
            old = top[...]
            new = jnp.maximum(old, lanes(jnp.max(scores, axis=1, keepdims=True), HD))
            factor = jnp.exp2(old - new)
            top[...] = new
            weights = jnp.exp2(scores - jnp.tile(new, (1, chunk // HD)))
            slopes = lax.dot_general(tq_q, keys_both, NT, preferred_element_type=jnp.float32)
            product = weights * slopes
            weights_b = weights.astype(jnp.bfloat16)
            product_b = product.astype(jnp.bfloat16)
            part = weights[:, 0:HD]
            part_shift = product[:, 0:HD]
            for k in range(1, chunk // HD):
                part = part + weights[:, k * HD : (k + 1) * HD]
                part_shift = part_shift + product[:, k * HD : (k + 1) * HD]
            total[...] = total[...] * factor + part
            shift[...] = shift[...] * factor + part_shift
            both[...] = both[...] * jnp.tile(factor, (1, 2)) + jnp.dot(
                weights_b, values_both, preferred_element_type=jnp.float32
            )
            mixed[...] = mixed[...] * factor + jnp.dot(
                product_b, values, preferred_element_type=jnp.float32
            )

        whole = ahead * run // chunk

        @pl.loop(0, whole)
        def _(index):
            visit(index, False)

        @pl.when((ahead + own) * run > whole * chunk)
        def _():
            visit(whole, True)

        if not last:
            for now, out in zip(state, outs):
                out[mine, :] = now[...]
            continue
        inverse = lanes(1.0 / jnp.sum(total[...], axis=1, keepdims=True), HD)
        shifted = lanes(jnp.sum(shift[...], axis=1, keepdims=True), HD) * (scale * inverse)
        context = both[:, 0:HD] * inverse
        tangent = (mixed[...] * scale + both[:, HD : 2 * HD]) * inverse - shifted * context
        out = outs[step]
        for h in range(group):
            cols = slice(h * HD, (h + 1) * HD)
            head = slice(h * run, (h + 1) * run)
            out[0:run, cols] = context[head].astype(out.dtype)
            out[run : 2 * run, cols] = tangent[head].astype(out.dtype)
    for copy in aside:
        copy.wait()


def finish_kernel(run, group, meta, query, tangent_query, *refs):
    height = group * run
    packs, before, outs, line = refs[:-8], refs[-8:-3], refs[-3:-1], refs[-1]
    scale = HD ** (-0.5)
    blocks = [(ref, begin) for ref in packs for begin in range(0, ref.shape[0], run)]
    for n, (ref, begin) in enumerate(blocks):
        place = pl.ds(pl.multiple_of(meta[4 + n] * run, run), run)
        line[place, :] = ref[begin : begin + run, :]
    chunk = line.shape[0]
    for step, out in enumerate(outs):
        half = meta[0] if step == 0 else 1 - meta[0]
        mine = slice(step * height, (step + 1) * height)
        rows = pl.ds(pl.multiple_of(half * run, run), run)
        ahead = meta[2 + half]
        q = [query[rows, h * HD : (h + 1) * HD] for h in range(group)]
        tq = [tangent_query[rows, h * HD : (h + 1) * HD] for h in range(group)]
        q = jnp.concatenate(q, axis=0)
        tq_q = jnp.concatenate([jnp.concatenate(tq, axis=0), q], axis=1)
        scores = lax.dot_general(q, line[:, 0:HD], NT, preferred_element_type=jnp.float32)
        slopes = lax.dot_general(
            tq_q, line[:, 0 : 2 * HD], NT, preferred_element_type=jnp.float32
        )
        col = lax.broadcasted_iota(jnp.int32, (height, chunk), 1)
        scores = jnp.where(col < ahead * run, scores * (scale * LOG2E), LOWEST)
        old, total, shift, both, mixed = (ref[mine, :] for ref in before)
        new = jnp.maximum(old, lanes(jnp.max(scores, axis=1, keepdims=True), HD))
        factor = jnp.exp2(old - new)
        weights = jnp.exp2(scores - jnp.tile(new, (1, chunk // HD)))
        product = weights * slopes
        total, shift = total * factor, shift * factor
        for k in range(chunk // HD):
            total = total + weights[:, k * HD : (k + 1) * HD]
            shift = shift + product[:, k * HD : (k + 1) * HD]
        weights_b, product_b = weights.astype(jnp.bfloat16), product.astype(jnp.bfloat16)
        both = both * jnp.tile(factor, (1, 2)) + jnp.dot(
            weights_b, line[:, 2 * HD : 4 * HD], preferred_element_type=jnp.float32
        )
        mixed = mixed * factor + jnp.dot(
            product_b, line[:, 2 * HD : 3 * HD], preferred_element_type=jnp.float32
        )
        inverse = lanes(1.0 / jnp.sum(total, axis=1, keepdims=True), HD)
        shifted = lanes(jnp.sum(shift, axis=1, keepdims=True), HD) * (scale * inverse)
        context = both[:, 0:HD] * inverse
        tangent = (mixed * scale + both[:, HD : 2 * HD]) * inverse - shifted * context
        for h in range(group):
            cols = slice(h * HD, (h + 1) * HD)
            head = slice(h * run, (h + 1) * run)
            out[0:run, cols] = context[head].astype(out.dtype)
            out[run : 2 * run, cols] = tangent[head].astype(out.dtype)


def finish(meta, query, tangent_query, packs, before):
    rows, width = query.shape
    count = sum(pack.shape[0] for pack in packs)
    out = jax.ShapeDtypeStruct((rows, width), jnp.bfloat16)
    return pl.pallas_call(
        functools.partial(finish_kernel, rows // 2, width // HD),
        out_shape=(out, out),
        in_specs=[SMEM] + [VMEM] * (2 + len(packs) + len(before)),
        out_specs=(VMEM,) * 2,
        scratch_shapes=[pltpu.VMEM((count, 4 * HD), jnp.bfloat16)],
        compiler_params=pltpu.CompilerParams(vmem_limit_bytes=16 * 2**20),
        cost_estimate=SMALL,
        name="finish",
    )(meta, query, tangent_query, *packs, *before)


def ranks(order, first, me, sources, own):
    place = order.reshape(-1, 2)[sources].reshape(-1)
    rank = jnp.sum(place[None, :] < place[:, None], axis=1, dtype=jnp.int32)
    ours = lax.dynamic_slice_in_dim(order, 2 * me, 2)
    ahead = jnp.sum(place[None, :] < ours[:, None], axis=1, dtype=jnp.int32)
    return jnp.concatenate([jnp.stack([first, jnp.int32(own)]), ahead, rank])


def attend(meta, query, tangent_query, packs, before=(), last=True, held=False, cut=()):
    rows, width = query.shape
    run, group = rows // 2, width // HD
    count = sum(pack.shape[0] for pack in packs)
    height = group * run
    chunk = 4 * run
    widths = (HD, HD, HD, 2 * HD, HD)
    if last:
        outs = (jax.ShapeDtypeStruct((rows, width), jnp.bfloat16),) * 2
    else:
        outs = tuple(jax.ShapeDtypeStruct((2 * height, w), jnp.float32) for w in widths)
    whole, parts = cut[:1], cut[1:]
    outs += tuple(jax.ShapeDtypeStruct((whole[0].shape[0], w), whole[0].dtype) for w in parts)
    sizes = (len(packs), len(before) // 5, last, held, len(parts), run, group, chunk)
    return pl.pallas_call(
        functools.partial(attend_kernel, sizes),
        out_shape=outs,
        in_specs=[SMEM, VMEM, VMEM]
        + [VMEM if held else ANY] * len(packs)
        + [VMEM] * len(before)
        + [ANY] * len(whole),
        out_specs=(VMEM,) * (len(outs) - len(parts)) + (ANY,) * len(parts),
        scratch_shapes=[pltpu.VMEM((count, 4 * HD), jnp.bfloat16)]
        + [pltpu.VMEM((height, w), jnp.float32) for w in widths]
        + [pltpu.SemaphoreType.DMA((count // run + len(parts),))],
        compiler_params=pltpu.CompilerParams(vmem_limit_bytes=16 * 2**20),
        cost_estimate=SMALL,
        name="attend_last" if last else "attend_early",
    )(meta, query, tangent_query, *(packs if held else in_hbm(packs)), *before, *whole)


def project_own_kernel(tile, left, weight, out, held, sems):
    count = weight.shape[1] // tile
    copies = []
    for n in range(count):
        cols = slice(n * tile, (n + 1) * tile)
        copies.append(pltpu.make_async_copy(weight.at[:, cols], held.at[n], sems.at[n]))
        copies[-1].start()
    rows = left[...]
    for n in range(count):
        copies[n].wait()
        out[:, n * tile : (n + 1) * tile] = jnp.dot(
            rows, held[n], preferred_element_type=jnp.float32
        ).astype(out.dtype)


def project_own(left, weight, tile=512):
    rows, depth = left.shape
    width = weight.shape[1]
    return pl.pallas_call(
        functools.partial(project_own_kernel, tile),
        out_shape=jax.ShapeDtypeStruct((rows, width), jnp.bfloat16),
        in_specs=[VMEM, HBM],
        out_specs=VMEM,
        scratch_shapes=[
            pltpu.VMEM((width // tile, depth, tile), jnp.bfloat16),
            pltpu.SemaphoreType.DMA((width // tile,)),
        ],
        compiler_params=pltpu.CompilerParams(vmem_limit_bytes=8 * 2**20),
        cost_estimate=SMALL,
        name="project_own",
    )(left, *in_hbm([weight]))


def columns_at(starts, counts, n, width):
    width = width // counts[n]
    at = sum(counts[:n])
    return [
        (
            slice(m * width, (m + 1) * width),
            pl.ds(pl.multiple_of(starts[at + m], HD), width),
        )
        for m in range(counts[n])
    ]


def project_other_kernel(counts, early, done, starts, left, partial, *refs):
    total = len(counts)
    pieces, refs = refs[:total], refs[total:]
    outs, refs = (refs[:2], refs[2:]) if done else ([], refs)
    sums, refs = list(pieces[:done]) + list(refs[: total - done]), refs[total - done :]
    held, (sems, out_sems) = refs[:early], refs[early:]
    run = left.shape[0] // 2
    rows = left[...]
    copies, stores = [], []
    for n in range(early):
        copies.append(pltpu.make_async_copy(pieces[done + n], held[n], sems.at[n]))
        copies[-1].start()

    def store(n):
        if not done:
            return
        for m, (here, cols) in enumerate(columns_at(starts, counts, n, sums[n].shape[1])):
            for k in range(2):
                stores.append(
                    pltpu.make_async_copy(
                        sums[n].at[k * run : (k + 1) * run, here],
                        outs[k].at[:, cols],
                        out_sems.at[sum(counts[:n]) + m, k],
                    )
                )
                stores[-1].start()

    for n in range(done):
        store(n)
    for n in list(range(done + early, total)) + list(range(done, done + early)):
        piece = pieces[n]
        if n < done + early:
            copies[n - done].wait()
            piece = held[n - done]
        other = jnp.dot(rows, piece[...], preferred_element_type=jnp.float32)
        other = other.astype(jnp.bfloat16).astype(jnp.float32)
        for here, cols in columns_at(starts, counts, n, piece.shape[1]):
            sums[n][:, here] = (partial[:, cols].astype(jnp.float32) + other[:, here]).astype(
                jnp.bfloat16
            )
        store(n)
    for copy in stores:
        copy.wait()


def project_other(places, left, partial, early, late, done=()):
    rows, width = left.shape[0], partial.shape[1]
    pieces = early + late
    counts = tuple(len(some) for some in places)
    starts = jnp.stack([start for some in places for start in some])
    sums = [jax.ShapeDtypeStruct((rows, piece.shape[1]), jnp.bfloat16) for piece in pieces]
    out = jax.ShapeDtypeStruct((rows // 2, width), jnp.bfloat16)
    scratch = [pltpu.VMEM(some.shape, some.dtype) for some in sums] if done else []
    scratch = scratch + [pltpu.VMEM(piece.shape, piece.dtype) for piece in early]
    return pl.pallas_call(
        functools.partial(project_other_kernel, counts, len(early), len(done)),
        out_shape=[out, out] if done else sums,
        in_specs=[SMEM, VMEM, VMEM] + [VMEM] * len(done) + [ANY] * len(early) + [VMEM] * len(late),
        out_specs=[HBM, HBM] if done else [VMEM] * len(sums),
        scratch_shapes=scratch
        + [pltpu.SemaphoreType.DMA((max(len(early), 1),))]
        + [pltpu.SemaphoreType.DMA((len(starts), 2))],
        compiler_params=pltpu.CompilerParams(vmem_limit_bytes=16 * 2**20),
        cost_estimate=SMALL if done else LARGE,
        name="project_last" if done else "project_other",
    )(starts, left, partial, *done, *in_hbm(early), *late)


def whole_program(
    query, key, value, tangent_query, tangent_key, tangent_value, out_weight, block_order, axes
):
    run = query.shape[0] // 2
    pack = jnp.concatenate([key, tangent_key, value, tangent_value], axis=1)
    gathered = lax.all_gather(pack, "ctx", axis=0, tiled=True)
    me = lax.axis_index("ctx").astype(jnp.int32)
    meta = ranks(block_order, jnp.int32(0), me, jnp.arange(axes["ctx"], dtype=jnp.int32), 1)
    first, second = attend(meta, query, tangent_query, [gathered])
    left = jnp.concatenate([first[:run], second[:run], first[run:], second[run:]], axis=0)
    partial = project_own(left, out_weight)
    both = jnp.concatenate([partial[: 2 * run], partial[2 * run :]], axis=1)
    summed = lax.psum_scatter(both, "head", scatter_dimension=0, tiled=True)
    width = out_weight.shape[1]
    return summed[:, :width], summed[:, width:]


def stage_kernel(widths, count, starts, weight, *refs):
    fields, outs, sems = refs[:count], refs[count:-1], refs[-1]
    moves = [(field, outs[0].at[:, n * HD : (n + 1) * HD]) for n, field in enumerate(fields)]
    parts = outs[1:] if fields else outs
    for part, some in zip(parts, widths):
        at = 0
        for width in some:
            cols = pl.ds(pl.multiple_of(starts[len(moves) - count], HD), width)
            moves.append((weight.at[:, cols], part.at[:, at : at + width]))
            at += width
    copies = [pltpu.make_async_copy(*move, sems.at[n]) for n, move in enumerate(moves)]
    for copy in copies:
        copy.start()
    for copy in copies:
        copy.wait()


def stage(starts, weight, widths, fields=()):
    shapes = [(weight.shape[0], sum(some)) for some in widths]
    if fields:
        shapes = [(fields[0].shape[0], HD * len(fields))] + shapes
    return pl.pallas_call(
        functools.partial(stage_kernel, widths, len(fields)),
        out_shape=[jax.ShapeDtypeStruct(shape, jnp.bfloat16) for shape in shapes],
        in_specs=[SMEM] + [HBM] * (1 + len(fields)),
        out_specs=[VMEM] * len(shapes),
        scratch_shapes=[pltpu.SemaphoreType.DMA((len(fields) + len(starts),))],
        compiler_params=pltpu.CompilerParams(vmem_limit_bytes=4 * 2**20),
        cost_estimate=SMALL,
        name="stage",
    )(jnp.stack(starts), *in_hbm((weight, *fields)))


def paired_program(
    query, key, value, tangent_query, tangent_key, tangent_value, out_weight, block_order, axes
):
    count = axes["ctx"]
    width = out_weight.shape[1]
    me = lax.axis_index("ctx").astype(jnp.int32)
    side = lax.axis_index("head").astype(jnp.int32)

    def swap(array, bits, *after):
        if after:
            array = lax.optimization_barrier((array,) + after)[0]
        return lax.ppermute(array, "ctx", [(i, i ^ bits) for i in range(count)])

    def cross(array):
        return lax.ppermute(array, "head", [(0, 1), (1, 0)])

    core, column, level = me & 1, (me >> 1) & 1, (me >> 2) & 1
    part = width // 16

    def by_level(level, core):
        return (2 * level + core) * part

    def by_column(column, core):
        return (4 + 2 * column + core) * part

    def by_core(core):
        return (8 + 4 * core) * part

    fields = (key, tangent_key, value, tangent_value)
    places = [by_level(level, core), by_column(column, core)]
    pack, shared = stage(places, out_weight, ((part, part),), fields)
    (direct,) = stage([by_core(core)], out_weight, ((4 * part,),))
    tie = lax.optimization_barrier
    bits = ([0, 1, 2, 4, 8, 3], [6, 12, 10, 7, 13, 11, 5, 9], [14, 15])
    metas = [
        ranks(block_order, 1 - side, me, me ^ jnp.array(some, jnp.int32), int(0 in some))
        for some in bits
    ]

    x0, z1, z2 = swap(pack, 2), swap(pack, 4), swap(pack, 8)
    shared = cross(shared)
    x0, pack = tie((x0, pack))
    c0, cx0 = swap(pack, 1), swap(x0, 1)
    metas, pack, c0, x0, cx0, z1, z2, direct = tie((metas, pack, c0, x0, cx0, z1, z2, direct))
    x1, x2, z3 = swap(z1, 2), swap(z2, 2), swap(z2, 4)
    direct = cross(direct)
    cz1, cz2 = swap(z1, 1), swap(z2, 1)
    packs = [pack, c0, x0, z1, z2, cx0]
    *state, level_part, column_part = attend(
        metas[0], query, tangent_query, packs, last=False, cut=(shared, part, part)
    )
    x1, x2, z3, cz1, cz2, shared, level_part, column_part, state = tie(
        (x1, x2, z3, cz1, cz2, shared, level_part, column_part, state)
    )
    x3 = swap(z3, 2)
    cx1, cz3, cx2 = swap(x1, 1), swap(z3, 1), swap(x2, 1)
    packs = [x1, z3, x2, cx1, cz3, cx2, cz1, cz2]
    state = attend(metas[1], query, tangent_query, packs, state, last=False, held=True)
    x3, shared, level_part, column_part, state = tie((x3, shared, level_part, column_part, state))
    level_part, column_part = swap(level_part, 4), swap(column_part, 2)
    cx3, shared_core = tie((swap(x3, 1), swap(shared, 1)))
    theirs, mine = finish(metas[2], query, tangent_query, [x3, cx3], state)

    other = cross(theirs)
    partial, level_part, column_part, direct = tie(
        (project_own(mine, out_weight), level_part, column_part, direct)
    )
    far = [swap(p, 1) for p in (direct, level_part, column_part)]
    near = [
        [by_level(level, core), by_column(column, core)],
        [by_level(level, 1 - core), by_column(column, 1 - core)],
        [by_level(1 - level, core)],
        [by_column(1 - column, core)],
        [by_core(core)],
    ]
    sums = project_other(
        near, other, partial, [shared, shared_core], [level_part, column_part, direct]
    )
    rest = [[by_core(1 - core)], [by_level(1 - level, 1 - core)], [by_column(1 - column, 1 - core)]]
    return tuple(project_other(near + rest, other, partial, [], far, sums))


def solution(mesh):
    axes = dict(mesh.shape)
    program = paired_program if axes == {"ctx": 16, "head": 2} else whole_program
    in_specs = (
        P("ctx", "head"),
        P("ctx", "head"),
        P("ctx", "head"),
        P("ctx", "head"),
        P("ctx", "head"),
        P("ctx", "head"),
        P("head", None),
        P(),
    )
    out_specs = (P(("ctx", "head"), None), P(("ctx", "head"), None))
    return jax.shard_map(
        functools.partial(program, axes=axes),
        mesh=mesh,
        in_specs=in_specs,
        out_specs=out_specs,
        check_vma=False,
    )
```

```python
import functools

import jax
import jax.numpy as jnp
from jax import lax
from jax.experimental import pallas as pl
from jax.experimental.pallas import tpu as pltpu
from jax.sharding import PartitionSpec as P

HD = 128
LOG2E = 1.4426950408889634
LOWEST = -1e30
VMEM = pl.BlockSpec(memory_space=pltpu.VMEM)
SMEM = pl.BlockSpec(memory_space=pltpu.SMEM)
ANY = pl.BlockSpec(memory_space=pl.ANY)
HBM = pl.BlockSpec(memory_space=pltpu.HBM)


def in_hbm(arrays):
    return [pltpu.with_memory_space_constraint(array, pltpu.HBM) for array in arrays]


def lanes(column, width):
    return jnp.broadcast_to(column, (column.shape[0], width))


SMALL = pl.CostEstimate(flops=1, bytes_accessed=1, transcendentals=0)
LARGE = pl.CostEstimate(flops=10**11, bytes_accessed=1, transcendentals=0)
NT = (((1,), (1,)), ((), ()))


def attend_kernel(sizes, meta, query, tangent_query, *refs):
    packs, carried, last, held, cuts, run, group, chunk = sizes
    height = group * run
    pack_refs, refs = refs[:packs], refs[packs:]
    before, refs = refs[: 5 * carried], refs[5 * carried :]
    whole_ref, refs = (refs[0], refs[1:]) if cuts else (None, refs)
    outs, refs = (refs[:2], refs[2:]) if last else (refs[:5], refs[5:])
    cut_refs, (line, top, total, shift, both, mixed, sems) = refs[:cuts], refs[cuts:]
    state = (top, total, shift, both, mixed)
    scale = HD ** (-0.5)

    aside, at = [], 0
    for n, ref in enumerate(cut_refs):
        source = whole_ref.at[:, at : at + ref.shape[1]]
        aside.append(pltpu.make_async_copy(source, ref, sems.at[line.shape[0] // run + n]))
        aside[-1].start()
        at += ref.shape[1]
    copies = []
    blocks = [(ref, begin) for ref in pack_refs for begin in range(0, ref.shape[0], run)]
    for n, (ref, begin) in enumerate(blocks):
        rows = pl.ds(pl.multiple_of(meta[4 + n] * run, run), run)
        block = ref.at[begin : begin + run, :]
        if held:
            line[rows, :] = block[...]
        else:
            copies.append(pltpu.make_async_copy(block, line.at[rows, :], sems.at[n]))
            copies[-1].start()
    for copy in copies:
        copy.wait()

    own = meta[1]
    for step in range(2):
        half = meta[0] if step == 0 else 1 - meta[0]
        ahead = meta[2 + half]
        mine = slice(step * height, (step + 1) * height)
        rows = pl.ds(pl.multiple_of(half * run, run), run)
        q = [query[rows, h * HD : (h + 1) * HD] for h in range(group)]
        tq = [tangent_query[rows, h * HD : (h + 1) * HD] for h in range(group)]
        q = jnp.concatenate(q, axis=0)
        tq_q = jnp.concatenate([jnp.concatenate(tq, axis=0), q], axis=1)
        if carried:
            for now, then in zip(state, before):
                now[...] = then[mine, :]
        else:
            top[...] = jnp.full(top.shape, LOWEST, jnp.float32)
            for now in state[1:]:
                now[...] = jnp.zeros(now.shape, jnp.float32)

        def visit(index, masked):
            cols = pl.ds(pl.multiple_of(index * chunk, chunk), chunk)
            keys = line[cols, 0:HD]
            keys_both = line[cols, 0 : 2 * HD]
            values = line[cols, 2 * HD : 3 * HD]
            values_both = line[cols, 2 * HD : 4 * HD]
            scores = lax.dot_general(q, keys, NT, preferred_element_type=jnp.float32)
            scores = scores * (scale * LOG2E)
            if masked:
                col = index * chunk + lax.broadcasted_iota(jnp.int32, (height, chunk), 1)
                row = lax.rem(lax.broadcasted_iota(jnp.int32, (height, chunk), 0), run)
                scores = jnp.where(col < ahead * run + (row + 1) * own, scores, LOWEST)
            old = top[...]
            new = jnp.maximum(old, lanes(jnp.max(scores, axis=1, keepdims=True), HD))
            factor = jnp.exp2(old - new)
            top[...] = new
            weights = jnp.exp2(scores - jnp.tile(new, (1, chunk // HD)))
            slopes = lax.dot_general(tq_q, keys_both, NT, preferred_element_type=jnp.float32)
            product = weights * slopes
            weights_b = weights.astype(jnp.bfloat16)
            product_b = product.astype(jnp.bfloat16)
            part = weights[:, 0:HD]
            part_shift = product[:, 0:HD]
            for k in range(1, chunk // HD):
                part = part + weights[:, k * HD : (k + 1) * HD]
                part_shift = part_shift + product[:, k * HD : (k + 1) * HD]
            total[...] = total[...] * factor + part
            shift[...] = shift[...] * factor + part_shift
            both[...] = both[...] * jnp.tile(factor, (1, 2)) + jnp.dot(
                weights_b, values_both, preferred_element_type=jnp.float32
            )
            mixed[...] = mixed[...] * factor + jnp.dot(
                product_b, values, preferred_element_type=jnp.float32
            )

        whole = ahead * run // chunk

        @pl.loop(0, whole)
        def _(index):
            visit(index, False)

        @pl.when((ahead + own) * run > whole * chunk)
        def _():
            visit(whole, True)

        if not last:
            for now, out in zip(state, outs):
                out[mine, :] = now[...]
            continue
        inverse = lanes(1.0 / jnp.sum(total[...], axis=1, keepdims=True), HD)
        shifted = lanes(jnp.sum(shift[...], axis=1, keepdims=True), HD) * (scale * inverse)
        context = both[:, 0:HD] * inverse
        tangent = (mixed[...] * scale + both[:, HD : 2 * HD]) * inverse - shifted * context
        out = outs[step]
        for h in range(group):
            cols = slice(h * HD, (h + 1) * HD)
            head = slice(h * run, (h + 1) * run)
            out[0:run, cols] = context[head].astype(out.dtype)
            out[run : 2 * run, cols] = tangent[head].astype(out.dtype)
    for copy in aside:
        copy.wait()


def finish_kernel(run, group, meta, query, tangent_query, *refs):
    height = group * run
    packs, before, outs, line = refs[:-8], refs[-8:-3], refs[-3:-1], refs[-1]
    scale = HD ** (-0.5)
    blocks = [(ref, begin) for ref in packs for begin in range(0, ref.shape[0], run)]
    for n, (ref, begin) in enumerate(blocks):
        place = pl.ds(pl.multiple_of(meta[4 + n] * run, run), run)
        line[place, :] = ref[begin : begin + run, :]
    chunk = line.shape[0]
    for step, out in enumerate(outs):
        half = meta[0] if step == 0 else 1 - meta[0]
        mine = slice(step * height, (step + 1) * height)
        rows = pl.ds(pl.multiple_of(half * run, run), run)
        ahead = meta[2 + half]
        q = [query[rows, h * HD : (h + 1) * HD] for h in range(group)]
        tq = [tangent_query[rows, h * HD : (h + 1) * HD] for h in range(group)]
        q = jnp.concatenate(q, axis=0)
        tq_q = jnp.concatenate([jnp.concatenate(tq, axis=0), q], axis=1)
        scores = lax.dot_general(q, line[:, 0:HD], NT, preferred_element_type=jnp.float32)
        slopes = lax.dot_general(
            tq_q, line[:, 0 : 2 * HD], NT, preferred_element_type=jnp.float32
        )
        col = lax.broadcasted_iota(jnp.int32, (height, chunk), 1)
        scores = jnp.where(col < ahead * run, scores * (scale * LOG2E), LOWEST)
        old, total, shift, both, mixed = (ref[mine, :] for ref in before)
        new = jnp.maximum(old, lanes(jnp.max(scores, axis=1, keepdims=True), HD))
        factor = jnp.exp2(old - new)
        weights = jnp.exp2(scores - jnp.tile(new, (1, chunk // HD)))
        product = weights * slopes
        total, shift = total * factor, shift * factor
        for k in range(chunk // HD):
            total = total + weights[:, k * HD : (k + 1) * HD]
            shift = shift + product[:, k * HD : (k + 1) * HD]
        weights_b, product_b = weights.astype(jnp.bfloat16), product.astype(jnp.bfloat16)
        both = both * jnp.tile(factor, (1, 2)) + jnp.dot(
            weights_b, line[:, 2 * HD : 4 * HD], preferred_element_type=jnp.float32
        )
        mixed = mixed * factor + jnp.dot(
            product_b, line[:, 2 * HD : 3 * HD], preferred_element_type=jnp.float32
        )
        inverse = lanes(1.0 / jnp.sum(total, axis=1, keepdims=True), HD)
        shifted = lanes(jnp.sum(shift, axis=1, keepdims=True), HD) * (scale * inverse)
        context = both[:, 0:HD] * inverse
        tangent = (mixed * scale + both[:, HD : 2 * HD]) * inverse - shifted * context
        for h in range(group):
            cols = slice(h * HD, (h + 1) * HD)
            head = slice(h * run, (h + 1) * run)
            out[0:run, cols] = context[head].astype(out.dtype)
            out[run : 2 * run, cols] = tangent[head].astype(out.dtype)


def finish(meta, query, tangent_query, packs, before):
    rows, width = query.shape
    count = sum(pack.shape[0] for pack in packs)
    out = jax.ShapeDtypeStruct((rows, width), jnp.bfloat16)
    return pl.pallas_call(
        functools.partial(finish_kernel, rows // 2, width // HD),
        out_shape=(out, out),
        in_specs=[SMEM] + [VMEM] * (2 + len(packs) + len(before)),
        out_specs=(VMEM,) * 2,
        scratch_shapes=[pltpu.VMEM((count, 4 * HD), jnp.bfloat16)],
        compiler_params=pltpu.CompilerParams(vmem_limit_bytes=16 * 2**20),
        cost_estimate=SMALL,
        name="finish",
    )(meta, query, tangent_query, *packs, *before)


def ranks(order, first, me, sources, own):
    place = order.reshape(-1, 2)[sources].reshape(-1)
    rank = jnp.sum(place[None, :] < place[:, None], axis=1, dtype=jnp.int32)
    ours = lax.dynamic_slice_in_dim(order, 2 * me, 2)
    ahead = jnp.sum(place[None, :] < ours[:, None], axis=1, dtype=jnp.int32)
    return jnp.concatenate([jnp.stack([first, jnp.int32(own)]), ahead, rank])


def attend(meta, query, tangent_query, packs, before=(), last=True, held=False, cut=()):
    rows, width = query.shape
    run, group = rows // 2, width // HD
    count = sum(pack.shape[0] for pack in packs)
    height = group * run
    chunk = 4 * run
    widths = (HD, HD, HD, 2 * HD, HD)
    if last:
        outs = (jax.ShapeDtypeStruct((rows, width), jnp.bfloat16),) * 2
    else:
        outs = tuple(jax.ShapeDtypeStruct((2 * height, w), jnp.float32) for w in widths)
    whole, parts = cut[:1], cut[1:]
    outs += tuple(jax.ShapeDtypeStruct((whole[0].shape[0], w), whole[0].dtype) for w in parts)
    sizes = (len(packs), len(before) // 5, last, held, len(parts), run, group, chunk)
    return pl.pallas_call(
        functools.partial(attend_kernel, sizes),
        out_shape=outs,
        in_specs=[SMEM, VMEM, VMEM]
        + [VMEM if held else ANY] * len(packs)
        + [VMEM] * len(before)
        + [ANY] * len(whole),
        out_specs=(VMEM,) * (len(outs) - len(parts)) + (ANY,) * len(parts),
        scratch_shapes=[pltpu.VMEM((count, 4 * HD), jnp.bfloat16)]
        + [pltpu.VMEM((height, w), jnp.float32) for w in widths]
        + [pltpu.SemaphoreType.DMA((count // run + len(parts),))],
        compiler_params=pltpu.CompilerParams(vmem_limit_bytes=16 * 2**20),
        cost_estimate=SMALL,
        name="attend_last" if last else "attend_early",
    )(meta, query, tangent_query, *(packs if held else in_hbm(packs)), *before, *whole)


def project_own_kernel(tile, relayed, left, weight, *refs):
    sources, out, targets = refs[:relayed], refs[relayed], refs[relayed + 1 : -2]
    held, sems = refs[-2:]
    count = weight.shape[1] // tile
    copies = []
    for n in range(count):
        cols = slice(n * tile, (n + 1) * tile)
        copies.append(pltpu.make_async_copy(weight.at[:, cols], held.at[n], sems.at[n]))
        copies[-1].start()
    for n, (source, target) in enumerate(zip(sources, targets)):
        copies.append(pltpu.make_async_copy(source, target, sems.at[count + n]))
        copies[-1].start()
    rows = left[...]
    for n in range(count):
        copies[n].wait()
        out[:, n * tile : (n + 1) * tile] = jnp.dot(
            rows, held[n], preferred_element_type=jnp.float32
        ).astype(out.dtype)
    for copy in copies[count:]:
        copy.wait()


def project_own(left, weight, pieces=(), tile=512):
    rows, depth = left.shape
    width = weight.shape[1]
    shapes = [(rows, width)] + [piece.shape for piece in pieces]
    return pl.pallas_call(
        functools.partial(project_own_kernel, tile, len(pieces)),
        out_shape=[jax.ShapeDtypeStruct(shape, jnp.bfloat16) for shape in shapes],
        in_specs=[VMEM, HBM] + [ANY] * len(pieces),
        out_specs=[VMEM] * len(shapes),
        scratch_shapes=[
            pltpu.VMEM((width // tile, depth, tile), jnp.bfloat16),
            pltpu.SemaphoreType.DMA((width // tile + len(pieces),)),
        ],
        compiler_params=pltpu.CompilerParams(vmem_limit_bytes=12 * 2**20),
        cost_estimate=SMALL,
        name="project_own",
    )(left, *in_hbm([weight, *pieces]))


def columns_at(starts, counts, n, width):
    width = width // counts[n]
    at = sum(counts[:n])
    return [
        (
            slice(m * width, (m + 1) * width),
            pl.ds(pl.multiple_of(starts[at + m], HD), width),
        )
        for m in range(counts[n])
    ]


def project_other_kernel(counts, early, done, starts, left, partial, *refs):
    total = len(counts)
    pieces, refs = refs[:total], refs[total:]
    outs, refs = (refs[:2], refs[2:]) if done else ([], refs)
    sums, refs = list(pieces[:done]) + list(refs[: total - done]), refs[total - done :]
    held, (sems, out_sems) = refs[:early], refs[early:]
    run = left.shape[0] // 2
    rows = left[...]
    copies, stores = [], []
    for n in range(early):
        copies.append(pltpu.make_async_copy(pieces[done + n], held[n], sems.at[n]))
        copies[-1].start()

    def store(n):
        if not done:
            return
        for m, (here, cols) in enumerate(columns_at(starts, counts, n, sums[n].shape[1])):
            for k in range(2):
                stores.append(
                    pltpu.make_async_copy(
                        sums[n].at[k * run : (k + 1) * run, here],
                        outs[k].at[:, cols],
                        out_sems.at[sum(counts[:n]) + m, k],
                    )
                )
                stores[-1].start()

    for n in range(done):
        store(n)
    for n in list(range(done + early, total)) + list(range(done, done + early)):
        piece = pieces[n]
        if n < done + early:
            copies[n - done].wait()
            piece = held[n - done]
        other = jnp.dot(rows, piece[...], preferred_element_type=jnp.float32)
        other = other.astype(jnp.bfloat16).astype(jnp.float32)
        for here, cols in columns_at(starts, counts, n, piece.shape[1]):
            sums[n][:, here] = (partial[:, cols].astype(jnp.float32) + other[:, here]).astype(
                jnp.bfloat16
            )
        store(n)
    for copy in stores:
        copy.wait()


def project_other(places, left, partial, early, late, done=()):
    rows, width = left.shape[0], partial.shape[1]
    pieces = early + late
    counts = tuple(len(some) for some in places)
    starts = jnp.stack([start for some in places for start in some])
    sums = [jax.ShapeDtypeStruct((rows, piece.shape[1]), jnp.bfloat16) for piece in pieces]
    out = jax.ShapeDtypeStruct((rows // 2, width), jnp.bfloat16)
    scratch = [pltpu.VMEM(some.shape, some.dtype) for some in sums] if done else []
    scratch = scratch + [pltpu.VMEM(piece.shape, piece.dtype) for piece in early]
    return pl.pallas_call(
        functools.partial(project_other_kernel, counts, len(early), len(done)),
        out_shape=[out, out] if done else sums,
        in_specs=[SMEM, VMEM, VMEM] + [VMEM] * len(done) + [ANY] * len(early) + [VMEM] * len(late),
        out_specs=[HBM, HBM] if done else [VMEM] * len(sums),
        scratch_shapes=scratch
        + [pltpu.SemaphoreType.DMA((max(len(early), 1),))]
        + [pltpu.SemaphoreType.DMA((len(starts), 2))],
        compiler_params=pltpu.CompilerParams(vmem_limit_bytes=16 * 2**20),
        cost_estimate=SMALL if done else LARGE,
        name="project_last" if done else "project_other",
    )(starts, left, partial, *done, *in_hbm(early), *late)


def whole_program(
    query, key, value, tangent_query, tangent_key, tangent_value, out_weight, block_order, axes
):
    run = query.shape[0] // 2
    pack = jnp.concatenate([key, tangent_key, value, tangent_value], axis=1)
    gathered = lax.all_gather(pack, "ctx", axis=0, tiled=True)
    me = lax.axis_index("ctx").astype(jnp.int32)
    meta = ranks(block_order, jnp.int32(0), me, jnp.arange(axes["ctx"], dtype=jnp.int32), 1)
    first, second = attend(meta, query, tangent_query, [gathered])
    left = jnp.concatenate([first[:run], second[:run], first[run:], second[run:]], axis=0)
    (partial,) = project_own(left, out_weight)
    both = jnp.concatenate([partial[: 2 * run], partial[2 * run :]], axis=1)
    summed = lax.psum_scatter(both, "head", scatter_dimension=0, tiled=True)
    width = out_weight.shape[1]
    return summed[:, :width], summed[:, width:]


def stage_kernel(widths, count, starts, weight, *refs):
    fields, outs, sems = refs[:count], refs[count:-1], refs[-1]
    moves = [(field, outs[0].at[:, n * HD : (n + 1) * HD]) for n, field in enumerate(fields)]
    parts = outs[1:] if fields else outs
    for part, some in zip(parts, widths):
        at = 0
        for width in some:
            cols = pl.ds(pl.multiple_of(starts[len(moves) - count], HD), width)
            moves.append((weight.at[:, cols], part.at[:, at : at + width]))
            at += width
    copies = [pltpu.make_async_copy(*move, sems.at[n]) for n, move in enumerate(moves)]
    for copy in copies:
        copy.start()
    for copy in copies:
        copy.wait()


def stage(starts, weight, widths, fields=()):
    shapes = [(weight.shape[0], sum(some)) for some in widths]
    if fields:
        shapes = [(fields[0].shape[0], HD * len(fields))] + shapes
    return pl.pallas_call(
        functools.partial(stage_kernel, widths, len(fields)),
        out_shape=[jax.ShapeDtypeStruct(shape, jnp.bfloat16) for shape in shapes],
        in_specs=[SMEM] + [HBM] * (1 + len(fields)),
        out_specs=[VMEM] * len(shapes),
        scratch_shapes=[pltpu.SemaphoreType.DMA((len(fields) + len(starts),))],
        compiler_params=pltpu.CompilerParams(vmem_limit_bytes=4 * 2**20),
        cost_estimate=SMALL,
        name="stage",
    )(jnp.stack(starts), *in_hbm((weight, *fields)))


def paired_program(
    query, key, value, tangent_query, tangent_key, tangent_value, out_weight, block_order, axes
):
    count = axes["ctx"]
    width = out_weight.shape[1]
    me = lax.axis_index("ctx").astype(jnp.int32)
    side = lax.axis_index("head").astype(jnp.int32)

    def swap(array, bits, *after):
        if after:
            array = lax.optimization_barrier((array,) + after)[0]
        return lax.ppermute(array, "ctx", [(i, i ^ bits) for i in range(count)])

    def cross(array):
        return lax.ppermute(array, "head", [(0, 1), (1, 0)])

    core, column, level = me & 1, (me >> 1) & 1, (me >> 2) & 1
    part = width // 16

    def by_level(level, core):
        return (2 * level + core) * part

    def by_column(column, core):
        return (4 + 2 * column + core) * part

    def by_core(core):
        return (8 + 4 * core) * part

    fields = (key, tangent_key, value, tangent_value)
    places = [by_level(level, core), by_column(column, core)]
    pack, shared = stage(places, out_weight, ((part, part),), fields)
    (direct,) = stage([by_core(core)], out_weight, ((4 * part,),))
    tie = lax.optimization_barrier
    bits = ([0, 1, 2, 4, 8, 3], [6, 12, 10, 7, 13, 11, 5, 9], [14, 15])
    metas = [
        ranks(block_order, 1 - side, me, me ^ jnp.array(some, jnp.int32), int(0 in some))
        for some in bits
    ]

    x0, z1, z2 = swap(pack, 2), swap(pack, 4), swap(pack, 8)
    shared = cross(shared)
    x0, pack = tie((x0, pack))
    c0, cx0 = swap(pack, 1), swap(x0, 1)
    metas, pack, c0, x0, cx0, z1, z2, direct = tie((metas, pack, c0, x0, cx0, z1, z2, direct))
    x1, x2, z3 = swap(z1, 2), swap(z2, 2), swap(z2, 4)
    direct = cross(direct)
    cz1, cz2 = swap(z1, 1), swap(z2, 1)
    packs = [pack, c0, x0, z1, z2, cx0]
    *state, level_part, column_part = attend(
        metas[0], query, tangent_query, packs, last=False, cut=(shared, part, part)
    )
    x1, x2, z3, cz1, cz2, shared, level_part, column_part, state = tie(
        (x1, x2, z3, cz1, cz2, shared, level_part, column_part, state)
    )
    x3 = swap(z3, 2)
    cx1, cz3, cx2 = swap(x1, 1), swap(z3, 1), swap(x2, 1)
    packs = [x1, z3, x2, cx1, cz3, cx2, cz1, cz2]
    state = attend(metas[1], query, tangent_query, packs, state, last=False, held=True)
    x3, shared, level_part, column_part, state = tie((x3, shared, level_part, column_part, state))
    level_part, column_part = swap(level_part, 4), swap(column_part, 2)
    cx3, shared_core = tie((swap(x3, 1), swap(shared, 1)))
    theirs, mine = finish(metas[2], query, tangent_query, [x3, cx3], state)

    other = cross(theirs)
    held = project_own(mine, out_weight, [shared, shared_core])
    held, level_part, column_part, direct = tie((held, level_part, column_part, direct))
    partial, shared, shared_core = held
    far = [swap(p, 1) for p in (direct, level_part, column_part)]
    near = [
        [by_level(level, core), by_column(column, core)],
        [by_level(level, 1 - core), by_column(column, 1 - core)],
        [by_level(1 - level, core)],
        [by_column(1 - column, core)],
        [by_core(core)],
    ]
    sums = project_other(
        near, other, partial, [], [shared, shared_core, level_part, column_part, direct]
    )
    rest = [[by_core(1 - core)], [by_level(1 - level, 1 - core)], [by_column(1 - column, 1 - core)]]
    return tuple(project_other(near + rest, other, partial, [], far, sums))


def solution(mesh):
    axes = dict(mesh.shape)
    program = paired_program if axes == {"ctx": 16, "head": 2} else whole_program
    in_specs = (
        P("ctx", "head"),
        P("ctx", "head"),
        P("ctx", "head"),
        P("ctx", "head"),
        P("ctx", "head"),
        P("ctx", "head"),
        P("head", None),
        P(),
    )
    out_specs = (P(("ctx", "head"), None), P(("ctx", "head"), None))
    return jax.shard_map(
        functools.partial(program, axes=axes),
        mesh=mesh,
        in_specs=in_specs,
        out_specs=out_specs,
        check_vma=False,
    )
```

```python
import functools

import jax
import jax.numpy as jnp
from jax import lax
from jax.experimental import pallas as pl
from jax.experimental.pallas import tpu as pltpu
from jax.sharding import PartitionSpec as P

HD = 128
LOG2E = 1.4426950408889634
LOWEST = -1e30
VMEM = pl.BlockSpec(memory_space=pltpu.VMEM)
SMEM = pl.BlockSpec(memory_space=pltpu.SMEM)
ANY = pl.BlockSpec(memory_space=pl.ANY)
HBM = pl.BlockSpec(memory_space=pltpu.HBM)


def in_hbm(arrays):
    return [pltpu.with_memory_space_constraint(array, pltpu.HBM) for array in arrays]


def lanes(column, width):
    return jnp.broadcast_to(column, (column.shape[0], width))


SMALL = pl.CostEstimate(flops=1, bytes_accessed=1, transcendentals=0)
LARGE = pl.CostEstimate(flops=10**11, bytes_accessed=1, transcendentals=0)
NT = (((1,), (1,)), ((), ()))


def attend_kernel(sizes, meta, query, tangent_query, *refs):
    packs, carried, last, held, cuts, run, group, chunk = sizes
    height = group * run
    pack_refs, refs = refs[:packs], refs[packs:]
    before, refs = refs[: 5 * carried], refs[5 * carried :]
    whole_ref, refs = (refs[0], refs[1:]) if cuts else (None, refs)
    outs, refs = (refs[:2], refs[2:]) if last else (refs[:5], refs[5:])
    cut_refs, (line, top, total, shift, both, mixed, sems) = refs[:cuts], refs[cuts:]
    state = (top, total, shift, both, mixed)
    scale = HD ** (-0.5)

    aside, at = [], 0
    for n, ref in enumerate(cut_refs):
        source = whole_ref.at[:, at : at + ref.shape[1]]
        aside.append(pltpu.make_async_copy(source, ref, sems.at[line.shape[0] // run + n]))
        aside[-1].start()
        at += ref.shape[1]
    copies = []
    blocks = [(ref, begin) for ref in pack_refs for begin in range(0, ref.shape[0], run)]
    for n, (ref, begin) in enumerate(blocks):
        rows = pl.ds(pl.multiple_of(meta[4 + n] * run, run), run)
        block = ref.at[begin : begin + run, :]
        if held:
            line[rows, :] = block[...]
        else:
            copies.append(pltpu.make_async_copy(block, line.at[rows, :], sems.at[n]))
            copies[-1].start()
    for copy in copies:
        copy.wait()

    own = meta[1]
    for step in range(2):
        half = meta[0] if step == 0 else 1 - meta[0]
        ahead = meta[2 + half]
        mine = slice(step * height, (step + 1) * height)
        rows = pl.ds(pl.multiple_of(half * run, run), run)
        q = [query[rows, h * HD : (h + 1) * HD] for h in range(group)]
        tq = [tangent_query[rows, h * HD : (h + 1) * HD] for h in range(group)]
        q = jnp.concatenate(q, axis=0)
        tq_q = jnp.concatenate([jnp.concatenate(tq, axis=0), q], axis=1)
        if carried:
            for now, then in zip(state, before):
                now[...] = then[mine, :]
        else:
            top[...] = jnp.full(top.shape, LOWEST, jnp.float32)
            for now in state[1:]:
                now[...] = jnp.zeros(now.shape, jnp.float32)

        def visit(index, masked):
            cols = pl.ds(pl.multiple_of(index * chunk, chunk), chunk)
            keys = line[cols, 0:HD]
            keys_both = line[cols, 0 : 2 * HD]
            values = line[cols, 2 * HD : 3 * HD]
            values_both = line[cols, 2 * HD : 4 * HD]
            scores = lax.dot_general(q, keys, NT, preferred_element_type=jnp.float32)
            scores = scores * (scale * LOG2E)
            if masked:
                col = index * chunk + lax.broadcasted_iota(jnp.int32, (height, chunk), 1)
                row = lax.rem(lax.broadcasted_iota(jnp.int32, (height, chunk), 0), run)
                scores = jnp.where(col < ahead * run + (row + 1) * own, scores, LOWEST)
            old = top[...]
            new = jnp.maximum(old, lanes(jnp.max(scores, axis=1, keepdims=True), HD))
            factor = jnp.exp2(old - new)
            top[...] = new
            weights = jnp.exp2(scores - jnp.tile(new, (1, chunk // HD)))
            slopes = lax.dot_general(tq_q, keys_both, NT, preferred_element_type=jnp.float32)
            product = weights * slopes
            weights_b = weights.astype(jnp.bfloat16)
            product_b = product.astype(jnp.bfloat16)
            part = weights[:, 0:HD]
            part_shift = product[:, 0:HD]
            for k in range(1, chunk // HD):
                part = part + weights[:, k * HD : (k + 1) * HD]
                part_shift = part_shift + product[:, k * HD : (k + 1) * HD]
            total[...] = total[...] * factor + part
            shift[...] = shift[...] * factor + part_shift
            both[...] = both[...] * jnp.tile(factor, (1, 2)) + jnp.dot(
                weights_b, values_both, preferred_element_type=jnp.float32
            )
            mixed[...] = mixed[...] * factor + jnp.dot(
                product_b, values, preferred_element_type=jnp.float32
            )

        whole = ahead * run // chunk

        @pl.loop(0, whole)
        def _(index):
            visit(index, False)

        @pl.when((ahead + own) * run > whole * chunk)
        def _():
            visit(whole, True)

        if not last:
            for now, out in zip(state, outs):
                out[mine, :] = now[...]
            continue
        inverse = lanes(1.0 / jnp.sum(total[...], axis=1, keepdims=True), HD)
        shifted = lanes(jnp.sum(shift[...], axis=1, keepdims=True), HD) * (scale * inverse)
        context = both[:, 0:HD] * inverse
        tangent = (mixed[...] * scale + both[:, HD : 2 * HD]) * inverse - shifted * context
        out = outs[step]
        for h in range(group):
            cols = slice(h * HD, (h + 1) * HD)
            head = slice(h * run, (h + 1) * run)
            out[0:run, cols] = context[head].astype(out.dtype)
            out[run : 2 * run, cols] = tangent[head].astype(out.dtype)
    for copy in aside:
        copy.wait()


def finish_kernel(run, group, meta, query, tangent_query, *refs):
    height = group * run
    packs, before, outs, line = refs[:-8], refs[-8:-3], refs[-3:-1], refs[-1]
    scale = HD ** (-0.5)
    blocks = [(ref, begin) for ref in packs for begin in range(0, ref.shape[0], run)]
    for n, (ref, begin) in enumerate(blocks):
        place = pl.ds(pl.multiple_of(meta[4 + n] * run, run), run)
        line[place, :] = ref[begin : begin + run, :]
    chunk = line.shape[0]
    qs, tqs, aheads = [], [], []
    for step in range(2):
        half = meta[0] if step == 0 else 1 - meta[0]
        rows = pl.ds(pl.multiple_of(half * run, run), run)
        aheads.append(meta[2 + half])
        qs += [query[rows, h * HD : (h + 1) * HD] for h in range(group)]
        tqs += [tangent_query[rows, h * HD : (h + 1) * HD] for h in range(group)]
    q = jnp.concatenate(qs, axis=0)
    tq_q = jnp.concatenate([jnp.concatenate(tqs, axis=0), q], axis=1)
    scores = lax.dot_general(q, line[:, 0:HD], NT, preferred_element_type=jnp.float32)
    slopes = lax.dot_general(tq_q, line[:, 0 : 2 * HD], NT, preferred_element_type=jnp.float32)
    col = lax.broadcasted_iota(jnp.int32, (2 * height, chunk), 1)
    row = lax.broadcasted_iota(jnp.int32, (2 * height, chunk), 0)
    limit = jnp.where(row < height, aheads[0] * run, aheads[1] * run)
    scores = jnp.where(col < limit, scores * (scale * LOG2E), LOWEST)
    old, total, shift, both, mixed = (ref[...] for ref in before)
    new = jnp.maximum(old, lanes(jnp.max(scores, axis=1, keepdims=True), HD))
    factor = jnp.exp2(old - new)
    weights = jnp.exp2(scores - jnp.tile(new, (1, chunk // HD)))
    product = weights * slopes
    total, shift = total * factor, shift * factor
    for k in range(chunk // HD):
        total = total + weights[:, k * HD : (k + 1) * HD]
        shift = shift + product[:, k * HD : (k + 1) * HD]
    weights_b, product_b = weights.astype(jnp.bfloat16), product.astype(jnp.bfloat16)
    both = both * jnp.tile(factor, (1, 2)) + jnp.dot(
        weights_b, line[:, 2 * HD : 4 * HD], preferred_element_type=jnp.float32
    )
    mixed = mixed * factor + jnp.dot(
        product_b, line[:, 2 * HD : 3 * HD], preferred_element_type=jnp.float32
    )
    inverse = lanes(1.0 / jnp.sum(total, axis=1, keepdims=True), HD)
    shifted = lanes(jnp.sum(shift, axis=1, keepdims=True), HD) * (scale * inverse)
    context = both[:, 0:HD] * inverse
    tangent = (mixed * scale + both[:, HD : 2 * HD]) * inverse - shifted * context
    for step, out in enumerate(outs):
        for h in range(group):
            cols = slice(h * HD, (h + 1) * HD)
            head = slice(step * height + h * run, step * height + (h + 1) * run)
            out[0:run, cols] = context[head].astype(out.dtype)
            out[run : 2 * run, cols] = tangent[head].astype(out.dtype)


def finish(meta, query, tangent_query, packs, before):
    rows, width = query.shape
    count = sum(pack.shape[0] for pack in packs)
    out = jax.ShapeDtypeStruct((rows, width), jnp.bfloat16)
    return pl.pallas_call(
        functools.partial(finish_kernel, rows // 2, width // HD),
        out_shape=(out, out),
        in_specs=[SMEM] + [VMEM] * (2 + len(packs) + len(before)),
        out_specs=(VMEM,) * 2,
        scratch_shapes=[pltpu.VMEM((count, 4 * HD), jnp.bfloat16)],
        compiler_params=pltpu.CompilerParams(vmem_limit_bytes=16 * 2**20),
        cost_estimate=SMALL,
        name="finish",
    )(meta, query, tangent_query, *packs, *before)


def ranks(order, first, me, sources, own):
    place = order.reshape(-1, 2)[sources].reshape(-1)
    rank = jnp.sum(place[None, :] < place[:, None], axis=1, dtype=jnp.int32)
    ours = lax.dynamic_slice_in_dim(order, 2 * me, 2)
    ahead = jnp.sum(place[None, :] < ours[:, None], axis=1, dtype=jnp.int32)
    return jnp.concatenate([jnp.stack([first, jnp.int32(own)]), ahead, rank])


def attend(meta, query, tangent_query, packs, before=(), last=True, held=False, cut=()):
    rows, width = query.shape
    run, group = rows // 2, width // HD
    count = sum(pack.shape[0] for pack in packs)
    height = group * run
    chunk = 4 * run
    widths = (HD, HD, HD, 2 * HD, HD)
    if last:
        outs = (jax.ShapeDtypeStruct((rows, width), jnp.bfloat16),) * 2
    else:
        outs = tuple(jax.ShapeDtypeStruct((2 * height, w), jnp.float32) for w in widths)
    whole, parts = cut[:1], cut[1:]
    outs += tuple(jax.ShapeDtypeStruct((whole[0].shape[0], w), whole[0].dtype) for w in parts)
    sizes = (len(packs), len(before) // 5, last, held, len(parts), run, group, chunk)
    return pl.pallas_call(
        functools.partial(attend_kernel, sizes),
        out_shape=outs,
        in_specs=[SMEM, VMEM, VMEM]
        + [VMEM if held else ANY] * len(packs)
        + [VMEM] * len(before)
        + [ANY] * len(whole),
        out_specs=(VMEM,) * (len(outs) - len(parts)) + (ANY,) * len(parts),
        scratch_shapes=[pltpu.VMEM((count, 4 * HD), jnp.bfloat16)]
        + [pltpu.VMEM((height, w), jnp.float32) for w in widths]
        + [pltpu.SemaphoreType.DMA((count // run + len(parts),))],
        compiler_params=pltpu.CompilerParams(vmem_limit_bytes=16 * 2**20),
        cost_estimate=SMALL,
        name="attend_last" if last else "attend_early",
    )(meta, query, tangent_query, *(packs if held else in_hbm(packs)), *before, *whole)


def project_own_kernel(tile, relayed, left, weight, *refs):
    sources, out, targets = refs[:relayed], refs[relayed], refs[relayed + 1 : -2]
    held, sems = refs[-2:]
    count = weight.shape[1] // tile
    copies = []
    for n in range(count):
        cols = slice(n * tile, (n + 1) * tile)
        copies.append(pltpu.make_async_copy(weight.at[:, cols], held.at[n], sems.at[n]))
        copies[-1].start()
    for n, (source, target) in enumerate(zip(sources, targets)):
        copies.append(pltpu.make_async_copy(source, target, sems.at[count + n]))
        copies[-1].start()
    rows = left[...]
    for n in range(count):
        copies[n].wait()
        out[:, n * tile : (n + 1) * tile] = jnp.dot(
            rows, held[n], preferred_element_type=jnp.float32
        ).astype(out.dtype)
    for copy in copies[count:]:
        copy.wait()


def project_own(left, weight, pieces=(), tile=512):
    rows, depth = left.shape
    width = weight.shape[1]
    shapes = [(rows, width)] + [piece.shape for piece in pieces]
    return pl.pallas_call(
        functools.partial(project_own_kernel, tile, len(pieces)),
        out_shape=[jax.ShapeDtypeStruct(shape, jnp.bfloat16) for shape in shapes],
        in_specs=[VMEM, HBM] + [ANY] * len(pieces),
        out_specs=[VMEM] * len(shapes),
        scratch_shapes=[
            pltpu.VMEM((width // tile, depth, tile), jnp.bfloat16),
            pltpu.SemaphoreType.DMA((width // tile + len(pieces),)),
        ],
        compiler_params=pltpu.CompilerParams(vmem_limit_bytes=12 * 2**20),
        cost_estimate=SMALL,
        name="project_own",
    )(left, *in_hbm([weight, *pieces]))


def columns_at(starts, counts, n, width):
    width = width // counts[n]
    at = sum(counts[:n])
    return [
        (
            slice(m * width, (m + 1) * width),
            pl.ds(pl.multiple_of(starts[at + m], HD), width),
        )
        for m in range(counts[n])
    ]


def project_other_kernel(counts, early, done, starts, left, partial, *refs):
    total = len(counts)
    pieces, refs = refs[:total], refs[total:]
    outs, refs = (refs[:2], refs[2:]) if done else ([], refs)
    sums, refs = list(pieces[:done]) + list(refs[: total - done]), refs[total - done :]
    held, (sems, out_sems) = refs[:early], refs[early:]
    run = left.shape[0] // 2
    rows = left[...]
    copies, stores = [], []
    for n in range(early):
        copies.append(pltpu.make_async_copy(pieces[done + n], held[n], sems.at[n]))
        copies[-1].start()

    def store(n):
        if not done:
            return
        for m, (here, cols) in enumerate(columns_at(starts, counts, n, sums[n].shape[1])):
            for k in range(2):
                stores.append(
                    pltpu.make_async_copy(
                        sums[n].at[k * run : (k + 1) * run, here],
                        outs[k].at[:, cols],
                        out_sems.at[sum(counts[:n]) + m, k],
                    )
                )
                stores[-1].start()

    for n in range(done):
        store(n)
    for n in list(range(done + early, total)) + list(range(done, done + early)):
        piece = pieces[n]
        if n < done + early:
            copies[n - done].wait()
            piece = held[n - done]
        other = jnp.dot(rows, piece[...], preferred_element_type=jnp.float32)
        other = other.astype(jnp.bfloat16).astype(jnp.float32)
        for here, cols in columns_at(starts, counts, n, piece.shape[1]):
            sums[n][:, here] = (partial[:, cols].astype(jnp.float32) + other[:, here]).astype(
                jnp.bfloat16
            )
        store(n)
    for copy in stores:
        copy.wait()


def project_other(places, left, partial, early, late, done=()):
    rows, width = left.shape[0], partial.shape[1]
    pieces = early + late
    counts = tuple(len(some) for some in places)
    starts = jnp.stack([start for some in places for start in some])
    sums = [jax.ShapeDtypeStruct((rows, piece.shape[1]), jnp.bfloat16) for piece in pieces]
    out = jax.ShapeDtypeStruct((rows // 2, width), jnp.bfloat16)
    scratch = [pltpu.VMEM(some.shape, some.dtype) for some in sums] if done else []
    scratch = scratch + [pltpu.VMEM(piece.shape, piece.dtype) for piece in early]
    return pl.pallas_call(
        functools.partial(project_other_kernel, counts, len(early), len(done)),
        out_shape=[out, out] if done else sums,
        in_specs=[SMEM, VMEM, VMEM] + [VMEM] * len(done) + [ANY] * len(early) + [VMEM] * len(late),
        out_specs=[HBM, HBM] if done else [VMEM] * len(sums),
        scratch_shapes=scratch
        + [pltpu.SemaphoreType.DMA((max(len(early), 1),))]
        + [pltpu.SemaphoreType.DMA((len(starts), 2))],
        compiler_params=pltpu.CompilerParams(vmem_limit_bytes=16 * 2**20),
        cost_estimate=SMALL if done else LARGE,
        name="project_last" if done else "project_other",
    )(starts, left, partial, *done, *in_hbm(early), *late)


def whole_program(
    query, key, value, tangent_query, tangent_key, tangent_value, out_weight, block_order, axes
):
    run = query.shape[0] // 2
    pack = jnp.concatenate([key, tangent_key, value, tangent_value], axis=1)
    gathered = lax.all_gather(pack, "ctx", axis=0, tiled=True)
    me = lax.axis_index("ctx").astype(jnp.int32)
    meta = ranks(block_order, jnp.int32(0), me, jnp.arange(axes["ctx"], dtype=jnp.int32), 1)
    first, second = attend(meta, query, tangent_query, [gathered])
    left = jnp.concatenate([first[:run], second[:run], first[run:], second[run:]], axis=0)
    (partial,) = project_own(left, out_weight)
    both = jnp.concatenate([partial[: 2 * run], partial[2 * run :]], axis=1)
    summed = lax.psum_scatter(both, "head", scatter_dimension=0, tiled=True)
    width = out_weight.shape[1]
    return summed[:, :width], summed[:, width:]


def stage_kernel(widths, count, starts, weight, *refs):
    fields, outs, sems = refs[:count], refs[count:-1], refs[-1]
    moves = [(field, outs[0].at[:, n * HD : (n + 1) * HD]) for n, field in enumerate(fields)]
    parts = outs[1:] if fields else outs
    for part, some in zip(parts, widths):
        at = 0
        for width in some:
            cols = pl.ds(pl.multiple_of(starts[len(moves) - count], HD), width)
            moves.append((weight.at[:, cols], part.at[:, at : at + width]))
            at += width
    copies = [pltpu.make_async_copy(*move, sems.at[n]) for n, move in enumerate(moves)]
    for copy in copies:
        copy.start()
    for copy in copies:
        copy.wait()


def stage(starts, weight, widths, fields=()):
    shapes = [(weight.shape[0], sum(some)) for some in widths]
    if fields:
        shapes = [(fields[0].shape[0], HD * len(fields))] + shapes
    return pl.pallas_call(
        functools.partial(stage_kernel, widths, len(fields)),
        out_shape=[jax.ShapeDtypeStruct(shape, jnp.bfloat16) for shape in shapes],
        in_specs=[SMEM] + [HBM] * (1 + len(fields)),
        out_specs=[VMEM] * len(shapes),
        scratch_shapes=[pltpu.SemaphoreType.DMA((len(fields) + len(starts),))],
        compiler_params=pltpu.CompilerParams(vmem_limit_bytes=4 * 2**20),
        cost_estimate=SMALL,
        name="stage",
    )(jnp.stack(starts), *in_hbm((weight, *fields)))


def paired_program(
    query, key, value, tangent_query, tangent_key, tangent_value, out_weight, block_order, axes
):
    count = axes["ctx"]
    width = out_weight.shape[1]
    me = lax.axis_index("ctx").astype(jnp.int32)
    side = lax.axis_index("head").astype(jnp.int32)

    def swap(array, bits, *after):
        if after:
            array = lax.optimization_barrier((array,) + after)[0]
        return lax.ppermute(array, "ctx", [(i, i ^ bits) for i in range(count)])

    def cross(array):
        return lax.ppermute(array, "head", [(0, 1), (1, 0)])

    core, column, level = me & 1, (me >> 1) & 1, (me >> 2) & 1
    part = width // 16

    def by_level(level, core):
        return (2 * level + core) * part

    def by_column(column, core):
        return (4 + 2 * column + core) * part

    def by_core(core):
        return (8 + 4 * core) * part

    fields = (key, tangent_key, value, tangent_value)
    places = [by_level(level, core), by_column(column, core)]
    pack, shared = stage(places, out_weight, ((part, part),), fields)
    (direct,) = stage([by_core(core)], out_weight, ((4 * part,),))
    tie = lax.optimization_barrier
    bits = ([0, 1, 2, 4, 8, 3], [6, 12, 10, 7, 13, 11, 5, 9], [14, 15])
    metas = [
        ranks(block_order, 1 - side, me, me ^ jnp.array(some, jnp.int32), int(0 in some))
        for some in bits
    ]

    x0, z1, z2 = swap(pack, 2), swap(pack, 4), swap(pack, 8)
    shared = cross(shared)
    x0, pack = tie((x0, pack))
    c0, cx0 = swap(pack, 1), swap(x0, 1)
    metas, pack, c0, x0, cx0, z1, z2, direct = tie((metas, pack, c0, x0, cx0, z1, z2, direct))
    x1, x2, z3 = swap(z1, 2), swap(z2, 2), swap(z2, 4)
    direct = cross(direct)
    cz1, cz2 = swap(z1, 1), swap(z2, 1)
    packs = [pack, c0, x0, z1, z2, cx0]
    *state, level_part, column_part = attend(
        metas[0], query, tangent_query, packs, last=False, cut=(shared, part, part)
    )
    x1, x2, z3, cz1, cz2, shared, level_part, column_part, state = tie(
        (x1, x2, z3, cz1, cz2, shared, level_part, column_part, state)
    )
    x3 = swap(z3, 2)
    cx1, cz3, cx2 = swap(x1, 1), swap(z3, 1), swap(x2, 1)
    packs = [x1, z3, x2, cx1, cz3, cx2, cz1, cz2]
    state = attend(metas[1], query, tangent_query, packs, state, last=False, held=True)
    x3, shared, level_part, column_part, state = tie((x3, shared, level_part, column_part, state))
    level_part, column_part = swap(level_part, 4), swap(column_part, 2)
    cx3, shared_core = tie((swap(x3, 1), swap(shared, 1)))
    theirs, mine = finish(metas[2], query, tangent_query, [x3, cx3], state)

    other = cross(theirs)
    held = project_own(mine, out_weight, [shared, shared_core])
    held, level_part, column_part, direct = tie((held, level_part, column_part, direct))
    partial, shared, shared_core = held
    far = [swap(p, 1) for p in (direct, level_part, column_part)]
    near = [
        [by_level(level, core), by_column(column, core)],
        [by_level(level, 1 - core), by_column(column, 1 - core)],
        [by_level(1 - level, core)],
        [by_column(1 - column, core)],
        [by_core(core)],
    ]
    sums = project_other(
        near, other, partial, [], [shared, shared_core, level_part, column_part, direct]
    )
    rest = [[by_core(1 - core)], [by_level(1 - level, 1 - core)], [by_column(1 - column, 1 - core)]]
    return tuple(project_other(near + rest, other, partial, [], far, sums))


def solution(mesh):
    axes = dict(mesh.shape)
    program = paired_program if axes == {"ctx": 16, "head": 2} else whole_program
    in_specs = (
        P("ctx", "head"),
        P("ctx", "head"),
        P("ctx", "head"),
        P("ctx", "head"),
        P("ctx", "head"),
        P("ctx", "head"),
        P("head", None),
        P(),
    )
    out_specs = (P(("ctx", "head"), None), P(("ctx", "head"), None))
    return jax.shard_map(
        functools.partial(program, axes=axes),
        mesh=mesh,
        in_specs=in_specs,
        out_specs=out_specs,
        check_vma=False,
    )
```
